32 devices in a mesh: tm: 16 (over z, y, core), space: 2 (over x).
Axes of the slice: x: 2, y: 2, z: 4, core: 2. Of those that a mesh axis runs over, the one named last changes fastest.
Arguments:
- initial: float32 [20, 128, 128], P('space'), may hold values from -6 to 6
- guess: float32 [16, 20, 128, 128], P('tm', 'space'), may hold values from -6 to 6
- diffusivity: float32 [20, 128, 128], P('space'), may hold values from 0.5 to 1
- velocity: float32 [3, 20, 128, 128], P(None, 'space'), may hold values from -1 to 1
Outputs:
- updated: float32 [16, 20, 128, 128], P('tm', 'space')
The draws below stay inside these ranges and needn't reach their ends.
All inputs are finite; a program needn't handle non-finite values.
Results may differ from the reference program's by a relative error of at most 0.00002.
Values sent between devices are 32-bit elements; how exact they have to be, the bound alone decides.
No kernel may reach another device: no remote copies, remote signals or barrier semaphores. Data moves between devices by JAX's collectives and lax.ppermute only.
A program may use at most 64 MiB of HBM per device.

```python
import math
import jax
import jax.numpy as jnp
from jax import lax

NX = 128
NY = 128
STEPS = 10
ITERS = 1
BLOCKS = 16
NZ = 20


def block_scale(own_key, shape, shards, low, largest):
    gain, own = 1.0, jax.random.fold_in(own_key, 6)
    for position, blocks in shards:
        heights = jnp.exp(jax.random.uniform(jax.random.fold_in(own, position), (blocks,), jnp.float32, low / len(shards), largest / len(shards)))
        gain = gain * jnp.repeat(heights, shape[position] // blocks).reshape([-1 if axis == position else 1 for axis in range(len(shape))])
    return gain


def noise(stream_key, shape, width, bound, shards=(), kind=jnp.bfloat16):
    entries = width * jax.random.normal(stream_key, shape, jnp.float32)
    if shards:
        entries = entries * block_scale(stream_key, shape, shards, -0.22, 0.18)
    return jnp.clip(entries, -bound, bound).astype(kind)


def setup_inputs(seed: int = 0) -> dict:
    key_list = jax.random.split(jax.random.key(seed), 5)
    initial = noise(key_list[0], (NZ, NX, NY), 1.0, 6.0, ((0, 2),), jnp.float32)
    guess = noise(key_list[1], (BLOCKS, NZ, NX, NY), 1.0, 6.0, ((0, 16), (1, 2)), jnp.float32)
    diffusivity = jnp.clip(jnp.exp(math.log(1.0) - 0.6931472 * jax.random.uniform(key_list[2], (NZ, NX, NY), jnp.float32) ** block_scale(key_list[2], (NZ, NX, NY), ((0, 2),), -0.2, 0.2)), 0.5, 1.0)
    velocity = jnp.clip(jax.random.uniform(key_list[3], (3, NZ, NX, NY), jnp.float32, -1.0, 1.0) * block_scale(key_list[3], (3, NZ, NX, NY), ((1, 2),), -0.4, 0.0), -1.0, 1.0)
    return {"initial": initial, "guess": guess, "diffusivity": diffusivity, "velocity": velocity}


FINE_DIFF = 0.01
FINE_ADV = 0.012
COARSE_DIFF = 0.1
COARSE_ADV = 0.12


def stencil(extended, diffus, pos_vel, neg_vel, diff_rate, adv_rate):
    center = extended[..., 1:-1, :, :]
    z_low = extended[..., :-2, :, :]
    z_high = extended[..., 2:, :, :]
    widths = [(0, 0)] * (center.ndim - 2) + [(1, 1), (1, 1)]
    padded = jnp.pad(center, widths)
    x_low = padded[..., :-2, 1:-1]
    x_high = padded[..., 2:, 1:-1]
    y_low = padded[..., 1:-1, :-2]
    y_high = padded[..., 1:-1, 2:]
    laplace = (z_low + z_high) + (x_low + x_high) + (y_low + y_high) - 6.0 * center
    advect = pos_vel[0] * (center - z_low) + neg_vel[0] * (z_high - center)
    advect = advect + pos_vel[1] * (center - x_low) + neg_vel[1] * (x_high - center)
    advect = advect + pos_vel[2] * (center - y_low) + neg_vel[2] * (y_high - center)
    return center + diff_rate * diffus * laplace - adv_rate * advect


def pad_depth(field):
    widths = [(0, 0)] * (field.ndim - 3) + [(1, 1), (0, 0), (0, 0)]
    return jnp.pad(field, widths)


def reference(initial, guess, diffusivity, velocity):
    pos_vel = jnp.maximum(velocity, 0.0)
    neg_vel = jnp.minimum(velocity, 0.0)
    state = guess

    def fine_step(index, field):
        return stencil(pad_depth(field), diffusivity, pos_vel, neg_vel, FINE_DIFF, FINE_ADV)

    def sweep_turn(carry, residue):
        fresh = stencil(pad_depth(carry), diffusivity, pos_vel, neg_vel, COARSE_DIFF, COARSE_ADV) + residue
        return fresh, fresh

    for cycle_index in range(ITERS):
        starts = jnp.concatenate([initial[None], state[:-1]], axis=0)
        fine_states = lax.fori_loop(0, STEPS, fine_step, starts)
        residue_all = fine_states - state
        _, corrections = lax.scan(sweep_turn, jnp.zeros_like(initial), residue_all)
        state = state + corrections
    return state
```

```python
import functools
import itertools

import jax
import jax.numpy as jnp
from jax import lax
from jax.experimental import pallas as pl
from jax.experimental.pallas import tpu as pltpu
from jax.sharding import PartitionSpec as P

STEPS = 10
FINE_DIFF = 0.01
FINE_ADV = 0.012
RATIO = 10.0
GROUP = 4
TILE = 8
VMEM_LIMIT = 56 * 1024 * 1024
VMEM = pl.BlockSpec(memory_space=pltpu.VMEM)
SMEM = pl.BlockSpec(memory_space=pltpu.SMEM)


def rounded(count):
    return -(-count // TILE) * TILE


class Plan:
    def __init__(self, shape, n_t, n_s):
        self.n_t, self.n_s = n_t, n_s
        self.depth, self.rows, self.lanes = shape
        self.layers = self.depth * n_s
        self.pairs = GROUP // 2
        self.groups = n_t // GROUP
        self.chunk = self.rows // (self.pairs * n_s)
        self.halo = rounded(STEPS + n_t - 2)
        self.width = self.width_of(self.halo)
        self.reach = [GROUP * d - 1 for d in range(1, self.groups)]
        self.far = rounded(self.reach[-1])

    def width_of(self, halo):
        return min(self.rows, self.chunk + 2 * rounded(halo))

    def start_of(self, chip, halo):
        return jnp.clip(chip * self.chunk - rounded(halo), 0, self.rows - self.width_of(halo))

    def box(self):
        return (self.layers + 2, self.width + 2 * TILE, self.lanes)

    def locate(self):
        self.t, self.s = lax.axis_index("tm"), lax.axis_index("space")
        self.core = self.t % 2
        self.y = (self.t // 2) % self.pairs
        self.z = self.t // GROUP
        self.chip = self.chip_at(self.y, self.s)
        self.base = self.start_of(self.chip, self.halo)
        places = [self.start_of(self.chip, h) - self.base for h in range(0, self.halo + 1, TILE)]
        self.scalars = jnp.stack([self.z, self.core, self.s, self.y, *places]).astype(jnp.int32)

    def chip_at(self, y, s):
        return s * self.pairs + y

    def partner(self, dy, ds):
        return (self.y + dy) % self.pairs, (self.s + ds) % self.n_s

    def send(self, value, dy=0, ds=0, dz=0, flip=False, only=None):
        pairs = []
        for t, s in itertools.product(range(self.n_t), range(self.n_s)):
            core, y, z = t % 2, (t // 2) % self.pairs, t // GROUP
            if z + dz >= self.groups or (only is not None and z != only):
                continue
            to_t = (z + dz) * GROUP + (y + dy) % self.pairs * 2 + (core ^ int(flip))
            pairs.append((t * self.n_s + s, to_t * self.n_s + (s + ds) % self.n_s))
        return lax.ppermute(value, ("tm", "space"), pairs)

    def others(self):
        return [(dy, ds) for ds in range(self.n_s) for dy in range(self.pairs) if dy or ds]


def cut(value, start, width, axis):
    return lax.dynamic_slice_in_dim(value, start, width, axis=axis)


def stepper(plan, scalars, coeff):
    def place(halo):
        return pl.multiple_of(scalars[4 + rounded(halo) // TILE], TILE)

    def step(source, target, halo, scale, plus=None, minus=None):
        first = place(halo)

        def strip(index, _):
            row = pl.multiple_of(first + index * TILE, TILE)
            inner = pl.ds(row, TILE)
            here = pl.ds(pl.multiple_of(row + TILE, TILE), TILE)
            low, mid = source[0, here, :], source[1, here, :]
            for layer in range(plan.layers):
                high = source[layer + 2, here, :]
                x_low = source[layer + 1, pl.ds(row + TILE - 1, TILE), :]
                x_high = source[layer + 1, pl.ds(row + TILE + 1, TILE), :]
                y_low = pltpu.roll(mid, 1, 1)
                y_high = pltpu.roll(mid, plan.lanes - 1, 1)
                change = (coeff[0, layer, inner, :] * mid + coeff[1, layer, inner, :] * low) + (
                    coeff[2, layer, inner, :] * high + coeff[3, layer, inner, :] * x_low
                )
                change = change + (coeff[4, layer, inner, :] * x_high + coeff[5, layer, inner, :] * y_low)
                change = change + coeff[6, layer, inner, :] * y_high
                fresh = mid + change if scale == 1.0 else mid + scale * change
                if plus is not None:
                    fresh = fresh + plus[layer + 1, here, :]
                if minus is not None:
                    fresh = fresh - minus[layer + 1, here, :]
                target[layer + 1, here, :] = fresh
                low, mid = mid, high
            return 0

        lax.fori_loop(0, plan.width_of(halo) // TILE, strip, 0)

    return step, place


def fine(step, source, one, two, halo, minus=None):
    now, turn = source, (one, two)
    for index in range(STEPS):
        last = index == STEPS - 1
        step(now, turn[index % 2], halo - 1 - index, 1.0, minus=minus if last else None)
        now = turn[index % 2]
    return now


def clear(*fields):
    for field in fields:
        field[...] = jnp.zeros_like(field)


def first_kernel(plan, count, *refs):
    refs = list(refs)
    scalars = refs.pop(0)
    guess = [refs.pop(0) for _ in range(count)]
    diff_own, vel_own = refs.pop(0), refs.pop(0)
    near = [refs.pop(0) for _ in range(plan.n_s - 1)]
    flipped = [refs.pop(0) for _ in range(plan.n_s - 1)]
    init_own = refs.pop(0)
    init_near = [refs.pop(0) for _ in range(plan.n_s - 1)]
    init_flipped = [refs.pop(0) for _ in range(plan.n_s - 1)]
    coeff, fields, keep, give, begun, one, two, three, four = refs
    z, core, s, y = (scalars[i] for i in range(4))
    half = plan.depth // 2
    width, lanes = plan.width, plan.lanes

    clear(one, two, three, four, fields)
    for (dy, ds), piece in zip([(0, 0), *plan.others()], guess):
        slot = lax.rem(y + plan.pairs - dy, plan.pairs)
        slab = lax.rem(s + plan.n_s - ds, plan.n_s)
        for layer in range(plan.depth):
            fields[slot, 1 + slab * plan.depth + layer, TILE : TILE + width, :] = piece[layer]

    lane = lax.broadcasted_iota(jnp.int32, (TILE, lanes), 1)

    def weights(layer, diff, vel):
        def strip(index, _):
            here = pl.ds(pl.multiple_of(index * TILE, TILE), TILE)
            spread = FINE_DIFF * diff(here)
            drift = [FINE_ADV * vel(k, here) for k in range(3)]
            total = 6.0 * spread
            for k in range(3):
                total = total + jnp.abs(drift[k])
                below = spread + jnp.maximum(drift[k], 0.0)
                above = spread - jnp.minimum(drift[k], 0.0)
                if k == 2:
                    below = jnp.where(lane == 0, 0.0, below)
                    above = jnp.where(lane == lanes - 1, 0.0, above)
                coeff[1 + 2 * k, layer, here, :] = below
                coeff[2 + 2 * k, layer, here, :] = above
            coeff[0, layer, here, :] = -total
            return 0

        lax.fori_loop(0, width // TILE, strip, 0)

    def own_layer(layer, _):
        weights(s * plan.depth + layer, lambda h: diff_own[layer, h, :], lambda k, h: vel_own[k, layer, h, :])
        return 0

    lax.fori_loop(0, plan.depth, own_layer, 0)
    for ds in range(1, plan.n_s):
        slab = lax.rem(s + plan.n_s - ds, plan.n_s)
        for part, which in ((near[ds - 1], core), (flipped[ds - 1], 1 - core)):

            def far_layer(layer, _, part=part, which=which, slab=slab):
                weights(
                    slab * plan.depth + which * half + layer,
                    lambda h: part[0, layer, h, :],
                    lambda k, h: part[1 + k, layer, h, :],
                )
                return 0

            lax.fori_loop(0, half, far_layer, 0)

    step, place = stepper(plan, scalars, coeff)
    reach = STEPS + plan.n_t - 2
    now, spare = fields.at[0], one
    for slot in range(1, plan.pairs):
        reach -= 1
        step(now, two, reach, RATIO)
        reach -= 1
        step(two, spare, reach, RATIO, plus=fields.at[slot])
        now, spare = spare, (three if spare is one else one)
    free = [f for f in (one, two, three, four) if f is not now]
    coarse = free.pop(0)
    step(now, coarse, reach - 1, RATIO)
    share = fine(step, now, free[0], free[1], reach, minus=coarse)
    reach -= STEPS
    others = [f for f in (one, two, three, four) if f is not share]

    far = plan.width_of(plan.far)
    begun[...] = jnp.zeros_like(begun)

    @pl.when(z == 0)
    def _():
        seed = others[2]
        for layer in range(plan.depth):
            seed[1 + s * plan.depth + layer, :, :] = init_own[layer]
        for ds in range(1, plan.n_s):
            slab = lax.rem(s + plan.n_s - ds, plan.n_s)
            for part, which in ((init_near[ds - 1], core), (init_flipped[ds - 1], 1 - core)):
                for layer in range(half):
                    seed[1 + slab * plan.depth + which * half + layer, :, :] = part[layer]
        value = fine(step, seed, others[0], others[1], STEPS + plan.n_t - 1)
        inner = pl.ds(place(plan.far) + TILE, far)
        for layer in range(plan.layers):
            begun[layer] = value[layer + 1, inner, :]

        @pl.when(core == 0)
        def _():
            left = plan.n_t - 1
            turn = [f for f in others if f is not value]
            now = value
            for index in range(GROUP - 1):
                left -= 1
                last = index == GROUP - 2
                step(now, share if last else turn[index % 2], left, RATIO, plus=share if last else None)
                now = turn[index % 2]

    @pl.when(core == 0)
    def _():
        step(share, others[0], reach - 1, RATIO)

    @pl.when(core != 0)
    def _():
        others[0][...] = share[...]

    total = others[0]
    inner = pl.ds(place(plan.far) + TILE, far)
    side = plan.layers // 2
    for layer in range(side):
        keep[layer] = total[1 + core * side + layer, inner, :]
        give[layer] = total[1 + (1 - core) * side + layer, inner, :]


def second_kernel(plan, scalars, coeff, fields, out, one, two, three):
    clear(one, two, three)
    step, place = stepper(plan, scalars, coeff)
    reach = STEPS + GROUP - 2
    for slot in range(plan.pairs):
        step(fields.at[slot], three, reach - 1, RATIO)
        result = fine(step, fields.at[slot], one, two, reach, minus=three)
        inner = pl.ds(place(TILE) + TILE, plan.width_of(TILE))
        for layer in range(plan.layers):
            out[slot, layer] = result[layer + 1, inner, :]


def third_kernel(plan, *refs):
    refs = list(refs)
    scalars, coeff, begun = refs.pop(0), refs.pop(0), refs.pop(0)
    steps = plan.groups - 1
    mine = [refs.pop(0) for _ in range(steps)]
    flipped = [refs.pop(0) for _ in range(steps)]
    w_mine, w_flipped = refs.pop(0), refs.pop(0)
    outs = [refs.pop(0) for _ in range(plan.pairs * plan.n_s)]
    one, two, three = refs
    core, s, y = scalars[1], scalars[2], scalars[3]
    side = plan.layers // 2
    clear(one, two, three)
    step, place = stepper(plan, scalars, coeff)

    def add_in(field, distance):
        reach = plan.reach[distance - 1]
        inner = pl.ds(place(reach) + TILE, plan.width_of(reach))
        for layer in range(side):
            for part, which in ((mine[distance - 1], core), (flipped[distance - 1], 1 - core)):
                index = 1 + which * side + layer
                field[index, inner, :] = field[index, inner, :] + part[layer]

    now, spare = one, two
    for distance in range(steps, 0, -1):
        add_in(now, distance)
        if distance > 1:
            left = plan.reach[distance - 1]
            for _ in range(GROUP):
                left -= 1
                step(now, spare, left, RATIO)
                now, spare = spare, now
    inner = pl.ds(place(plan.far) + TILE, plan.width_of(plan.far))
    for layer in range(plan.layers):
        now[layer + 1, inner, :] = now[layer + 1, inner, :] + begun[layer]

    def write(block, field):
        slot = block // 2
        rows = pl.ds(place(0) + TILE, plan.chunk)

        @pl.when(core == block % 2)
        def _():
            for index, (dy, ds) in enumerate([(0, 0), *plan.others()]):

                @pl.when(lax.rem(y + dy, plan.pairs) == slot)
                def _():
                    slab = lax.rem(s + ds, plan.n_s)
                    for layer in range(plan.depth):
                        outs[index][layer] = field[1 + slab * plan.depth + layer, rows, :]

    write(0, now)
    band = pl.ds(place(TILE) + TILE, plan.width_of(TILE))
    left = GROUP - 1
    for block in range(1, GROUP):
        left -= 1
        parity, slot = (block - 1) % 2, (block - 1) // 2

        @pl.when(core == parity)
        def _():
            for layer in range(plan.layers):
                three[layer + 1, band, :] = w_mine[slot, layer]

        @pl.when(core != parity)
        def _():
            for layer in range(plan.layers):
                three[layer + 1, band, :] = w_flipped[slot, layer]

        step(now, spare, left, RATIO, plus=three)
        now, spare = spare, now
        write(block, now)


def place_kernel(plan, scalars, *refs):
    out, pieces = refs[-1], refs[:-1]
    s, y = scalars[2], scalars[3]
    for (dy, ds), piece in zip([(0, 0), *plan.others()], pieces):
        chip = lax.rem(s + plan.n_s - ds, plan.n_s) * plan.pairs + lax.rem(y + plan.pairs - dy, plan.pairs)
        rows = pl.ds(pl.multiple_of(chip * plan.chunk, TILE), plan.chunk)
        out[:, rows, :] = piece[...]


def call(kernel, name, outs, scratch, *args):
    return pl.pallas_call(
        kernel,
        out_shape=outs,
        in_specs=[SMEM] + [VMEM] * (len(args) - 1),
        out_specs=jax.tree.map(lambda _: VMEM, outs),
        scratch_shapes=scratch,
        compiler_params=pltpu.CompilerParams(vmem_limit_bytes=VMEM_LIMIT),
        name=name,
    )(*args)


def by_regions(initial, guess, diffusivity, velocity):
    plan = Plan(diffusivity.shape, lax.axis_size("tm"), lax.axis_size("space"))
    plan.locate()
    f32 = functools.partial(jax.ShapeDtypeStruct, dtype=jnp.float32)
    depth, lanes, width, half = plan.depth, plan.lanes, plan.width, plan.depth // 2
    state = guess[0]

    def start_at(dy, ds):
        return plan.start_of(plan.chip_at(*plan.partner(dy, ds)), plan.halo)

    pieces = [cut(state, plan.base, width, 1)]
    for dy, ds in plan.others():
        pieces.append(plan.send(cut(state, start_at(dy, ds), width, 1), dy, ds))

    near, flipped = [], []
    init_near, init_flipped = [], []
    padded = jnp.pad(initial, ((0, 0), (TILE, TILE), (0, 0)))
    for ds in range(1, plan.n_s):
        start = start_at(0, ds)
        diff = lax.dynamic_slice(diffusivity, (plan.core * half, start, 0), (half, width, lanes))
        vel = lax.dynamic_slice(velocity, (0, plan.core * half, start, 0), (3, half, width, lanes))
        part = plan.send(jnp.concatenate([diff[None], vel]), ds=ds)
        near.append(part)
        flipped.append(plan.send(part, flip=True))
        part = lax.dynamic_slice(padded, (plan.core * half, start, 0), (half, width + 2 * TILE, lanes))
        part = plan.send(part, ds=ds, only=0)
        init_near.append(part)
        init_flipped.append(plan.send(part, flip=True, only=0))
    init_own = cut(padded, plan.base, width + 2 * TILE, 1)

    far = plan.width_of(plan.far)
    side = plan.layers // 2
    box = pltpu.VMEM(plan.box(), jnp.float32)
    coeff, fields, keep, give, begun = call(
        functools.partial(first_kernel, plan, len(pieces)),
        "group_total",
        [
            f32((7, plan.layers, width, lanes)),
            f32((plan.pairs, *plan.box())),
            f32((side, far, lanes)),
            f32((side, far, lanes)),
            f32((plan.layers, far, lanes)),
        ],
        [box] * 4,
        plan.scalars,
        *pieces,
        cut(diffusivity, plan.base, width, 1),
        cut(velocity, plan.base, width, 2),
        *near,
        *flipped,
        init_own,
        *init_near,
        *init_flipped,
    )
    total = keep + plan.send(give, flip=True)
    far_start = plan.start_of(plan.chip, plan.far)
    mine = []
    for distance, reach in enumerate(plan.reach, 1):
        part = cut(total, plan.start_of(plan.chip, reach) - far_start, plan.width_of(reach), 1)
        mine.append(plan.send(part, dz=distance))
    (w_mine,) = call(
        functools.partial(second_kernel, plan),
        "block_terms",
        [f32((plan.pairs, plan.layers, plan.width_of(TILE), lanes))],
        [box] * 3,
        plan.scalars,
        coeff,
        fields,
    )
    w_flipped = plan.send(w_mine, flip=True)
    results = call(
        functools.partial(third_kernel, plan),
        "block_ends",
        [f32((depth, plan.chunk, lanes))] * (plan.pairs * plan.n_s),
        [box] * 3,
        plan.scalars,
        coeff,
        begun,
        *mine,
        *[plan.send(part, flip=True) for part in mine],
        w_mine,
        w_flipped,
    )
    back = [results[0]]
    for (dy, ds), part in zip(plan.others(), results[1:]):
        back.append(plan.send(part, dy, ds))
    (out,) = call(
        functools.partial(place_kernel, plan),
        "place_rows",
        [f32((depth, plan.rows, lanes))],
        [],
        plan.scalars,
        *back,
    )
    return out[None]


def padded_2(cells, sides, width):
    for axis, dim in sides:
        count = lax.axis_size(axis)
        ends = count - 1
        head = lax.slice_in_dim(cells, 0, width, axis=dim)
        tail = lax.slice_in_dim(cells, cells.shape[dim] - width, cells.shape[dim], axis=dim)
        cells = jnp.concatenate(
            [
                lax.ppermute(tail, axis, [(i, (i + 1) % count) for i in range(ends)]),
                cells,
                lax.ppermute(head, axis, [((i + 1) % count, i) for i in range(ends)]),
            ],
            axis=dim,
        )
    return cells


def from_behind(value, axis, steps):
    count = lax.axis_size(axis)
    first, last = (max(0, -steps), min(count, count - steps))
    return lax.ppermute(value, axis, [(source, source + steps) for source in range(first, last)])


def stencil(extended, diffus, pos_vel, neg_vel, diff_rate, adv_rate):
    center = extended[..., 1:-1, :, :]
    z_low = extended[..., :-2, :, :]
    z_high = extended[..., 2:, :, :]
    widths = [(0, 0)] * (center.ndim - 2) + [(1, 1), (1, 1)]
    padded = jnp.pad(center, widths)
    x_low = padded[..., :-2, 1:-1]
    x_high = padded[..., 2:, 1:-1]
    y_low = padded[..., 1:-1, :-2]
    y_high = padded[..., 1:-1, 2:]
    laplace = z_low + z_high + (x_low + x_high) + (y_low + y_high) - 6.0 * center
    advect = pos_vel[0] * (center - z_low) + neg_vel[0] * (z_high - center)
    advect = advect + pos_vel[1] * (center - x_low) + neg_vel[1] * (x_high - center)
    advect = advect + pos_vel[2] * (center - y_low) + neg_vel[2] * (y_high - center)
    return center + diff_rate * diffus * laplace - adv_rate * advect


def by_slabs(initial, guess, diffusivity, velocity):
    pos_vel = jnp.maximum(velocity, 0.0)
    neg_vel = jnp.minimum(velocity, 0.0)
    depth = diffusivity.shape[0]
    total_depth = depth * lax.axis_size("space")
    first_row = lax.axis_index("space") * depth
    block_index = lax.axis_index("tm")
    block_count = lax.axis_size("tm")
    state = guess[0]
    stacked = jnp.concatenate([diffusivity[None], velocity], axis=0)
    wide_coeff = padded_2(stacked, (("space", 1),), STEPS)
    wide_diff = wide_coeff[0]
    wide_pos = jnp.maximum(wide_coeff[1:], 0.0)
    wide_neg = jnp.minimum(wide_coeff[1:], 0.0)
    previous_end = from_behind(state, "tm", 1)
    starts = jnp.where(block_index == 0, initial, previous_end)
    current = padded_2(starts, (("space", 0),), STEPS)
    for step_index in range(STEPS):
        margin = STEPS - step_index - 1
        rows = depth + 2 * margin
        lower = step_index + 1
        fresh = stencil(
            current,
            wide_diff[lower : lower + rows],
            wide_pos[:, lower : lower + rows],
            wide_neg[:, lower : lower + rows],
            FINE_DIFF,
            FINE_ADV,
        )
        global_rows = first_row - margin + lax.iota(jnp.int32, rows)
        inside = (global_rows >= 0) & (global_rows < total_depth)
        current = jnp.where(inside[:, None, None], fresh, 0.0)
    residue = current - state

    def sweep_turn(index, carry):
        previous = from_behind(carry, "tm", 1)
        beside_all = padded_2(previous, (("space", 0),), 1)
        return stencil(beside_all, diffusivity, pos_vel, neg_vel, RATIO * FINE_DIFF, RATIO * FINE_ADV) + residue

    correction = lax.fori_loop(0, block_count, sweep_turn, jnp.zeros_like(state))
    state = state + correction
    return state[None]


def fits(plan):
    if plan.n_t % GROUP or plan.n_t < 2 * GROUP or plan.depth % 2 or plan.rows % (plan.pairs * plan.n_s * TILE):
        return False
    return 4 * 20 * plan.layers * plan.width * plan.lanes <= VMEM_LIMIT


def per_device(initial, guess, diffusivity, velocity):
    plan = Plan(diffusivity.shape, lax.axis_size("tm"), lax.axis_size("space"))
    way = by_regions if fits(plan) else by_slabs
    return way(initial, guess, diffusivity, velocity)


def solution(mesh):
    in_specs = (
        P("space", None, None),
        P("tm", "space", None, None),
        P("space", None, None),
        P(None, "space", None, None),
    )
    out_specs = P("tm", "space", None, None)
    return jax.shard_map(per_device, mesh=mesh, in_specs=in_specs, out_specs=out_specs, check_vma=False)
```

```python
import functools
import itertools
import math

import jax
import jax.numpy as jnp
from jax import lax
from jax.experimental import pallas as pl
from jax.experimental.pallas import tpu as pltpu
from jax.sharding import PartitionSpec as P

STEPS = 10
FINE_DIFF = 0.01
FINE_ADV = 0.012
RATIO = 10.0
GROUP = 4
TILE = 8
LANES = 128
SPARE_BYTES = 4 * 1024 * 1024
VMEM_BYTES = 56 * 1024 * 1024
VMEM = pl.BlockSpec(memory_space=pltpu.VMEM)
HBM = pl.BlockSpec(memory_space=pltpu.HBM)


def rounded(count):
    return -(-count // TILE) * TILE


class Plan:
    def __init__(self, shape, n_t, n_s):
        self.n_t, self.n_s = n_t, n_s
        self.depth, self.rows, self.lanes = shape
        self.layers = self.depth * n_s
        self.pairs = GROUP // 2
        self.groups = n_t // GROUP
        self.chunk = self.rows // (self.pairs * n_s)
        self.halo = rounded(STEPS + n_t - 2)
        self.width = self.width_of(self.halo)
        self.wide = min(self.rows, self.width + 2 * TILE)
        self.reach = [GROUP * d - 1 for d in range(1, self.groups)]
        self.far = self.reach[-1]
        self.side = self.layers // 2
        self.others = [(dy, ds) for ds in range(n_s) for dy in range(self.pairs) if dy or ds]
        spans = [(y * n_s * self.chunk, (y + 1) * n_s * self.chunk) for y in range(self.pairs)]
        self.span = max(min(self.rows, end + self.halo) - max(0, start - self.halo) for start, end in spans)
        self.mid = STEPS + GROUP - 1

    def width_of(self, halo):
        return min(self.rows, self.chunk + 2 * rounded(halo))

    def start_of(self, chip, halo):
        start = jnp.clip(chip * self.chunk - rounded(halo), 0, self.rows - self.width_of(halo))
        return pl.multiple_of(start, TILE)

    def wide_start(self, chip):
        start = jnp.clip(chip * self.chunk - self.halo - TILE, 0, self.rows - self.wide)
        return pl.multiple_of(start, TILE)

    def span_start(self, y):
        start = jnp.clip(y * self.n_s * self.chunk - self.halo, 0, self.rows - self.span)
        return pl.multiple_of(start, TILE)

    def box(self):
        return (self.layers + 2, self.width + 2 * TILE, self.lanes)

    def send(self, value, dy=0, ds=0, dz=0, flip=False, swap=False, first=False):
        pairs = []
        for t, s in itertools.product(range(self.n_t), range(self.n_s)):
            core, y, z = t % 2, (t // 2) % self.pairs, t // GROUP
            to_z = z ^ 1 if swap else z + dz
            if to_z >= self.groups or (first and (z or core)):
                continue
            to_t = to_z * GROUP + (y + dy) % self.pairs * 2 + (core ^ int(flip))
            pairs.append((t * self.n_s + s, to_t * self.n_s + (s + ds) % self.n_s))
        return lax.ppermute(value, ("tm", "space"), pairs)


class Place:
    def __init__(self, plan):
        self.plan = plan
        t = lax.axis_index("tm")
        self.s = lax.axis_index("space")
        self.core = lax.rem(t, 2)
        self.y = lax.rem(lax.div(t, 2), plan.pairs)
        self.z = lax.div(t, GROUP)
        self.chip = self.y * plan.n_s + self.s
        self.base = plan.start_of(self.chip, plan.halo)

    def ahead(self, dy, ds):
        plan = self.plan
        return lax.rem(self.y + dy, plan.pairs) * plan.n_s + lax.rem(self.s + ds, plan.n_s)

    def behind(self, dy, ds):
        plan = self.plan
        return lax.rem(self.y + plan.pairs - dy, plan.pairs), lax.rem(self.s + plan.n_s - ds, plan.n_s)

    def inner(self, halo):
        return pl.multiple_of(self.plan.start_of(self.chip, halo) - self.base, TILE)


def fetch(sem, copies):
    started = [pltpu.make_async_copy(source, target, sem.at[index]) for index, (source, target) in enumerate(copies)]
    for copy in started:
        copy.start()
    return started


def shifts(lanes):
    row = lax.broadcasted_iota(jnp.int32, (2 * lanes, 2 * lanes), 0)
    row = jnp.where(row >= lanes, row - lanes, row)
    column = lax.broadcasted_iota(jnp.int32, (2 * lanes, 2 * lanes), 1)
    up = jnp.where(row == column - 1, 1.0, 0.0)
    down = jnp.where(row == column - lanes + 1, 1.0, 0.0)
    return jnp.where(column < lanes, up, down).astype(jnp.bfloat16)


def with_shifts(plan, body):
    count = plan.layers // 2

    def run(*sums):
        matrix = shifts(plan.lanes)
        for unit in range(2):
            pltpu.matmul_push_rhs(matrix, 0, unit)
            pltpu.matmul_acc_lhs(sums[unit], jnp.zeros((2 * TILE, 2 * plan.lanes), jnp.bfloat16), load_staged_rhs=0)
            pltpu.matmul_pop(sums[unit])
        body((sums[:count], sums[count:]))

    pl.run_scoped(
        run,
        *[pltpu.ACC(i % count % 2)((2 * TILE, 2 * plan.lanes), jnp.float32) for i in range(2 * count)],
    )


def stepper(plan, place, coeff, sums):
    count = plan.layers // 2

    def step(source, target, halo, scale, plus=None, minus=None):
        first = place.inner(halo)
        strips = plan.width_of(halo) // TILE

        def rows(index):
            return pl.multiple_of(first + index * TILE, TILE)

        def shift(index, which, pair):
            here = pl.ds(pl.multiple_of(rows(index) + TILE, TILE), TILE)
            value = source[pl.ds(1 + 2 * pair, 2), here, :].reshape(2 * TILE, plan.lanes)
            high = value.astype(jnp.bfloat16)
            rest = (value - high.astype(jnp.float32)).astype(jnp.bfloat16)
            pltpu.matmul_acc_lhs(sums[which][pair], jnp.concatenate([high, rest], axis=1))

        def strip(index, which, later):
            row = rows(index)
            inner = pl.ds(row, TILE)
            here = pl.ds(pl.multiple_of(row + TILE, TILE), TILE)
            low, mid = source[0, here, :], source[1, here, :]
            for layer in range(plan.layers):
                if layer % 2 == 0:
                    shift(later, 1 - which, layer // 2)
                    moved = pltpu.matmul_pop(sums[which][layer // 2])
                part = moved[layer % 2 * TILE : (layer % 2 + 1) * TILE]
                high = source[layer + 2, here, :]
                x_low = source[layer + 1, pl.ds(row + TILE - 1, TILE), :]
                x_high = source[layer + 1, pl.ds(row + TILE + 1, TILE), :]
                change = (coeff[0, layer, inner, :] * mid + coeff[1, layer, inner, :] * low) + (
                    coeff[2, layer, inner, :] * high + coeff[3, layer, inner, :] * x_low
                )
                change = change + (coeff[4, layer, inner, :] * x_high + coeff[5, layer, inner, :] * part[:, : plan.lanes])
                change = change + coeff[6, layer, inner, :] * part[:, plan.lanes :]
                fresh = mid + change if scale == 1.0 else mid + scale * change
                if plus is not None:
                    fresh = fresh + plus(layer, row)
                if minus is not None:
                    fresh = fresh - minus(layer, row)
                target[layer + 1, here, :] = fresh
                low, mid = mid, high

        for pair in range(count):
            shift(0, 0, pair)

        def two(index, _):
            strip(2 * index, 0, jnp.minimum(2 * index + 1, strips - 1))
            strip(jnp.minimum(2 * index + 1, strips - 1), 1, jnp.minimum(2 * index + 2, strips - 1))
            return 0

        lax.fori_loop(0, -(-strips // 2), two, 0)
        for pair in range(count):
            pltpu.matmul_pop(sums[0][pair])

    return step


def field_at(field):
    return lambda layer, row: field[layer + 1, pl.ds(pl.multiple_of(row + TILE, TILE), TILE), :]


def fine(step, source, one, two, halo, minus=None):
    now, turn = source, (one, two)
    for index in range(STEPS):
        last = index == STEPS - 1
        step(now, turn[index % 2], halo - 1 - index, 1.0, minus=minus if last else None)
        now = turn[index % 2]
    return now


def clear(plan, *fields):
    for field in fields:
        edge = jnp.zeros((TILE, plan.lanes), jnp.float32)
        for layer in range(plan.layers + 2):
            field[layer, :TILE, :] = edge
            field[layer, TILE + plan.width :, :] = edge
        for layer in (0, plan.layers + 1):
            field[layer] = jnp.zeros_like(field[layer])


def first_cut_kernel(plan, guess, diff, vel, *refs):
    place = Place(plan)
    sem = refs[-1]
    coeffs, blocks = refs[: plan.n_s - 1], refs[plan.n_s - 1 : -1]
    which = place.core * 2 + lax.rem(place.z, 2)

    def source(ds, array):
        rows = pl.ds(plan.start_of(place.ahead(0, ds), plan.halo), plan.width)
        return diff.at[:, rows, :] if array is None else vel.at[array, :, rows, :]

    for ds, target in enumerate(coeffs, 1):

        @pl.when(which == 0)
        def _(ds=ds, target=target):
            pltpu.make_async_copy(source(ds, None), target, sem.at[ds - 1]).start()

        @pl.when(which > 0)
        def _(ds=ds, target=target):
            pltpu.make_async_copy(source(ds, jnp.maximum(which - 1, 0)), target, sem.at[ds - 1]).start()

    copies = []
    for dy, target in enumerate(blocks, 1):
        start = plan.span_start(lax.rem(place.y + dy, plan.pairs))
        copies.append(pltpu.make_async_copy(guess.at[0, :, pl.ds(start, plan.span), :], target, sem.at[plan.n_s - 2 + dy]))
    for copy in copies:
        copy.start()
    for ds, target in enumerate(coeffs, 1):
        pltpu.make_async_copy(source(ds, None), target, sem.at[ds - 1]).wait()
    for copy in copies:
        copy.wait()


def second_cut_kernel(plan, guess, initial, diff, vel, *refs):
    place = Place(plan)
    refs, sem = refs[:-1], refs[-1]
    count = plan.n_s - 1
    blocks, inits = refs[:count], refs[count : 2 * count]
    guess_own, initial_own, coeff_own = refs[2 * count :]
    copies = []
    for ds, target in enumerate(blocks, 1):
        start = plan.start_of(place.ahead(0, ds), plan.halo)
        copies.append((guess.at[0, :, pl.ds(start, plan.width), :], target))
    for ds, target in enumerate(inits, 1):
        start = plan.wide_start(place.ahead(0, ds))
        copies.append((initial.at[:, pl.ds(start, plan.wide), :], target))
    rows = pl.ds(place.base, plan.width)
    copies.append((guess.at[0, :, rows, :], guess_own))
    copies.append((initial.at[:, pl.ds(plan.wide_start(place.chip), plan.wide), :], initial_own))
    copies.append((diff.at[:, rows, :], coeff_own.at[0]))
    copies.append((vel.at[:, :, rows, :], coeff_own.at[pl.ds(1, 3)]))
    for copy in fetch(sem, copies):
        copy.wait()


def mix_kernel(plan, *refs):
    place = Place(plan)
    count = plan.n_s - 1
    own, others, outs = refs[:count], refs[count:-count], refs[-count:]
    for ds, (block, out) in enumerate(zip(own, outs), 1):
        out[0] = block[...]
        start = plan.start_of(place.ahead(0, ds), plan.halo) - plan.span_start(place.y)
        for slot, other in enumerate(others, 1):
            out[slot] = other[:, pl.ds(pl.multiple_of(start, TILE), plan.width), :]


def field_kernel(plan, own, *refs):
    place = Place(plan)
    beside, far = refs[: plan.pairs - 1], refs[plan.pairs - 1 : -2]
    fields, given = refs[-2:]
    clear(plan, *[fields.at[slot] for slot in range(plan.pairs)])
    rows = pl.ds(TILE, plan.width)
    given_rows = pl.ds(place.inner(plan.mid), plan.width_of(plan.mid))

    def take(dy, ds, read):
        slot, slab = place.behind(dy, ds)

        def layer(index, _):
            value = read(index)
            fields[slot, 1 + slab * plan.depth + index, rows, :] = value
            return 0

        lax.fori_loop(0, plan.depth, layer, 0)

    take(0, 0, lambda index: own[index])
    start = pl.multiple_of(place.base - plan.span_start(place.y), TILE)
    for dy, block in enumerate(beside, 1):
        take(dy, 0, lambda index, block=block: block[index, pl.ds(start, plan.width), :])
    for ds, blocks in enumerate(far, 1):
        for dy in range(plan.pairs):
            take(dy, ds, lambda index, blocks=blocks, dy=dy: blocks[dy, index])
    for slot in range(plan.pairs):
        for layer in range(plan.layers):
            given[slot, layer] = fields[slot, 1 + layer, pl.ds(pl.multiple_of(given_rows.start + TILE, TILE), given_rows.size), :]


def weight_kernel(plan, coeff_own, window, *refs):
    refs = list(refs)
    near, init_near = [], []
    for _ in range(plan.n_s - 1):
        near.append(refs[:4])
        init_near.append(refs[4])
        del refs[:5]
    coeff, seed, ahead, parts, one = refs
    place = Place(plan)
    z, core, s = place.z, place.core, place.s
    even = lax.rem(z, 2)
    for ds, (mine, swapped, flipped, both) in enumerate(near, 1):
        for ref, array in (
            (mine, 2 * core + even),
            (swapped, 2 * core + 1 - even),
            (flipped, 2 * (1 - core) + even),
            (both, 2 * (1 - core) + 1 - even),
        ):
            parts[ds - 1, array] = ref[...]
    lane = lax.broadcasted_iota(jnp.int32, (plan.width, plan.lanes), 1)
    for ds in range(plan.n_s):
        slab = place.behind(0, ds)[1]

        def layer_weights(layer, _, ds=ds, slab=slab):
            index = slab * plan.depth + layer
            held = parts.at[ds - 1] if ds else coeff_own
            spread = FINE_DIFF * held[0, layer]
            total = 6.0 * spread
            for k in range(3):
                drift = FINE_ADV * held[1 + k, layer]
                total = total + jnp.abs(drift)
                below = spread + jnp.maximum(drift, 0.0)
                above = spread - jnp.minimum(drift, 0.0)
                if k == 2:
                    below = jnp.where(lane == 0, 0.0, below)
                    above = jnp.where(lane == plan.lanes - 1, 0.0, above)
                coeff[1 + 2 * k, index] = below
                coeff[2 + 2 * k, index] = above
            coeff[0, index] = -total
            return 0

        lax.fori_loop(0, plan.depth, layer_weights, 0)

    @pl.when((z == 0) & (core == 0))
    def _():
        seed[...] = jnp.zeros_like(seed)
        offset = lax.div(place.base - plan.wide_start(place.chip), TILE) - 1

        def fill(target_layer, source):
            for index in range(plan.width // TILE + 2):
                strip = index + offset
                inside = (strip >= 0) & (strip < plan.wide // TILE)
                held = pl.ds(pl.multiple_of(jnp.clip(strip, 0, plan.wide // TILE - 1) * TILE, TILE), TILE)
                value = jnp.where(inside, source[held, :], 0.0)
                seed[target_layer, index * TILE : (index + 1) * TILE, :] = value

        for ds in range(plan.n_s):
            slab = place.behind(0, ds)[1]
            held = init_near[ds - 1] if ds else window

            def take(layer, _, held=held, slab=slab):
                fill(1 + slab * plan.depth + layer, held.at[layer])
                return 0

            lax.fori_loop(0, plan.depth, take, 0)

        def body(sums):
            step = stepper(plan, place, coeff, sums)
            clear(plan, ahead, one)
            now, turn, reach = seed, (ahead, one), STEPS + plan.n_t - 1
            for index in range(GROUP - 1):
                reach -= 1
                step(now, turn[index % 2], reach, RATIO)
                now = turn[index % 2]
            if now is one:
                ahead[...] = one[...]

        with_shifts(plan, body)


def total_kernel(plan, coeff, ahead, fields, keep, give, one, two, three):
    place = Place(plan)
    z, core = place.z, place.core
    clear(plan, one, two, three)

    def body(sums):
        step = stepper(plan, place, coeff, sums)
        reach = STEPS + plan.n_t - 2
        now = fields.at[0]
        for slot in range(1, plan.pairs):
            reach -= 1
            step(now, two, reach, RATIO)
            now, spare = two, (one if slot % 2 else three)
            reach -= 1
            step(now, spare, reach, RATIO, plus=field_at(fields.at[slot]))
            now = spare
        free = [f for f in (one, two, three) if f is not now]
        coarse = free.pop()
        step(now, coarse, reach - 1, RATIO)

        @pl.when((z == 0) & (core == 0))
        def _():
            for layer in range(1, plan.layers + 1):
                now[layer] = now[layer] + ahead[layer]

        share = fine(step, now, free[0], now, reach, minus=field_at(coarse))
        reach -= STEPS
        total = free[0]

        @pl.when(core == 0)
        def _():
            step(share, total, reach - 1, RATIO)

        @pl.when(core != 0)
        def _():
            for layer in range(1, plan.layers + 1):
                total[layer] = share[layer]

        inner = pl.ds(pl.multiple_of(place.inner(plan.far) + TILE, TILE), plan.width_of(plan.far))
        for layer in range(plan.side):
            keep[layer] = total[1 + core * plan.side + layer, inner, :]
            give[layer] = total[1 + (1 - core) * plan.side + layer, inner, :]

    with_shifts(plan, body)


def part_kernel(plan, keep, got, *outs):
    place = Place(plan)
    for reach, out in zip(plan.reach, outs):
        start = pl.multiple_of(place.inner(reach) - place.inner(plan.far), TILE)
        rows = pl.ds(start, plan.width_of(reach))
        for layer in range(plan.side):
            out[layer] = keep[layer, rows, :] + got[layer, rows, :]


def term_kernel(plan, coeff, fields, flipped, seed, terms, begun, one, two, three):
    place = Place(plan)
    core = place.core
    clear(plan, one, two, three)
    middle = pl.ds(pl.multiple_of(place.inner(plan.mid) + TILE, TILE), plan.width_of(plan.mid))

    def body(sums):
        step = stepper(plan, place, coeff, sums)

        def term(source, coarse, other, reach, out, halo):
            step(source, coarse, reach - 1, RATIO)
            result = fine(step, source, other, source, reach, minus=field_at(coarse))
            rows = pl.ds(pl.multiple_of(place.inner(halo) + TILE, TILE), plan.width_of(halo))
            for layer in range(plan.layers):
                out[layer] = result[layer + 1, rows, :]

        def load(block, target):
            @pl.when(core == block % 2)
            def _():
                target[...] = fields[block // 2]

            @pl.when(core != block % 2)
            def _():
                for layer in range(plan.layers):
                    target[layer + 1, middle, :] = flipped[block // 2, layer]

        def block_term(block):
            load(0, one)
            left = STEPS + block - 1
            now, spare = one, two
            for before in range(1, block):
                load(before, three)
                left -= 1
                step(now, spare, left, RATIO, plus=field_at(three))
                now, spare = spare, now
            term(now, three, spare, left, terms.at[block // 2], 0)

        for block in range(GROUP):

            @pl.when(core == block % 2)
            def _(block=block):
                if block == 0:
                    terms[0] = jnp.zeros_like(terms[0])
                else:
                    block_term(block)

        started = (place.z == 0) & (core == 0)

        @pl.when(started)
        def _():
            one[...] = seed[...]
            result = fine(step, one, two, one, STEPS + GROUP - 1)
            rows = pl.ds(pl.multiple_of(place.inner(TILE) + TILE, TILE), plan.width_of(TILE))
            for layer in range(plan.layers):
                begun[layer] = result[layer + 1, rows, :]

        @pl.when(jnp.logical_not(started))
        def _():
            begun[...] = jnp.zeros_like(begun)

    with_shifts(plan, body)


def start_kernel(plan, coeff, begun, *refs):
    *totals, out, one, two = refs
    place = Place(plan)
    clear(plan, one, two)

    def body(sums):
        step = stepper(plan, place, coeff, sums)
        now, spare = one, two
        now[...] = jnp.zeros_like(now)
        for distance in range(len(totals), 0, -1):

            @pl.when(place.z >= distance)
            def _(distance=distance):
                reach = plan.reach[distance - 1]
                rows = pl.ds(pl.multiple_of(place.inner(reach) + TILE, TILE), plan.width_of(reach))
                for layer in range(plan.side):
                    index = 1 + place.core * plan.side + layer
                    now[index, rows, :] = now[index, rows, :] + totals[distance - 1][layer]
                if distance > 1:
                    for turn in range(GROUP):
                        source, target = (now, spare) if turn % 2 == 0 else (spare, now)
                        step(source, target, reach - 1 - turn, RATIO)

        rows = pl.ds(pl.multiple_of(place.inner(TILE) + TILE, TILE), plan.width_of(TILE))
        for layer in range(plan.layers):
            out[layer] = now[layer + 1, rows, :] + begun[layer]

    with_shifts(plan, body)


def end_kernel(plan, coeff, share, other, terms, *refs):
    *outs, one, two = refs
    place = Place(plan)
    core, s, y = place.core, place.s, place.y
    clear(plan, one, two)
    chunk = pl.ds(pl.multiple_of(place.inner(0) + TILE, TILE), plan.chunk)
    rows = pl.ds(pl.multiple_of(place.inner(TILE) + TILE, TILE), plan.width_of(TILE))
    for layer in range(plan.layers):
        one[layer + 1, rows, :] = share[layer] + other[layer]

    def write(block, field):
        @pl.when(core == block % 2)
        def _():
            for out, (dy, ds) in zip(outs, [(0, 0), *plan.others]):

                @pl.when(lax.rem(y + dy, plan.pairs) == block // 2)
                def _(out=out, ds=ds):
                    slab = lax.rem(s + ds, plan.n_s)
                    for layer in range(plan.depth):
                        value = field[1 + slab * plan.depth + layer, chunk, :]
                        out[layer] = value + terms[block // 2, slab * plan.depth + layer] if block else value

    def body(sums):
        step = stepper(plan, place, coeff, sums)
        now, spare = one, two
        write(0, now)
        for block in range(1, GROUP):
            step(now, spare, GROUP - 1 - block, RATIO)
            now, spare = spare, now
            write(block, now)

    with_shifts(plan, body)


def place_kernel(plan, *refs):
    place = Place(plan)
    out, sem, pieces = refs[-2], refs[-1], refs[:-2]
    copies = []
    for (dy, ds), piece in zip([(0, 0), *plan.others], pieces):
        y, s = place.behind(dy, ds)
        rows = pl.ds(pl.multiple_of((y * plan.n_s + s) * plan.chunk, TILE), plan.chunk)
        copies.append((piece, out.at[:, rows, :]))
    for copy in fetch(sem, copies):
        copy.wait()


def call(plan, kernel, micros, outs, scratch, *args, copies=0, whole=0, out_whole=False):
    spaces = [pltpu.HBM] * whole + [pltpu.VMEM] * (len(args) - whole)
    args = [pltpu.with_memory_space_constraint(arg, space) for arg, space in zip(args, spaces)]
    held = pltpu.HBM if out_whole else pltpu.VMEM
    needed = sum(4 * math.prod(shape) for shape in scratch)
    return pl.pallas_call(
        functools.partial(kernel, plan),
        out_shape=[held(shape, jnp.float32) for shape in outs],
        in_specs=[HBM] * whole + [VMEM] * (len(args) - whole),
        out_specs=[HBM if out_whole else VMEM] * len(outs),
        scratch_shapes=[pltpu.VMEM(shape, jnp.float32) for shape in scratch]
        + ([pltpu.SemaphoreType.DMA((copies,))] if copies else []),
        compiler_params=pltpu.CompilerParams(vmem_limit_bytes=needed + SPARE_BYTES),
        cost_estimate=pl.CostEstimate(flops=0, transcendentals=0, bytes_accessed=int(micros * 3.6e6)),
        name=kernel.__name__,
    )(*args)


def by_regions(initial, guess, diffusivity, velocity):
    plan = Plan(diffusivity.shape, lax.axis_size("tm"), lax.axis_size("space"))
    depth, lanes, width = plan.depth, plan.lanes, plan.width
    box, sides = plan.box(), plan.n_s - 1
    band, far = plan.width_of(TILE), plan.width_of(plan.far)
    window, piece = (depth, plan.wide, lanes), (depth, width, lanes)

    cuts = call(
        plan,
        first_cut_kernel,
        2,
        [piece] * sides + [(depth, plan.span, lanes)] * (plan.pairs - 1),
        [],
        guess,
        diffusivity,
        velocity,
        copies=sides + plan.pairs - 1,
        whole=3,
    )
    got = [plan.send(part, ds=ds) for ds, part in enumerate(cuts[:sides], 1)]
    got += [plan.send(part, dy=dy) for dy, part in enumerate(cuts[sides:], 1)]
    cuts = call(
        plan,
        second_cut_kernel,
        2,
        [piece] * sides + [window] * sides + [piece, window, (4, *piece)],
        [],
        guess,
        initial,
        diffusivity,
        velocity,
        copies=2 * sides + 4,
        whole=4,
    )
    own_sent, inits, (guess_own, initial_own, coeff_own) = cuts[:sides], cuts[sides : 2 * sides], cuts[2 * sides :]
    got = lax.optimization_barrier(got)
    coeffs, beside = got[:sides], got[sides:]
    mixed = call(plan, mix_kernel, 0.3, [(plan.pairs, *piece)] * sides, [], *own_sent, *beside)
    distant = [plan.send(part, ds=ds) for ds, part in enumerate(mixed, 1)]
    inits = [plan.send(init, ds=ds, first=True) for ds, init in enumerate(inits, 1)]
    swapped = []
    for part in coeffs:
        swapped.append(plan.send(part, swap=True))
        swapped.append(plan.send(part, flip=True))
        swapped.append(plan.send(part, swap=True, flip=True))
    got = lax.optimization_barrier((*distant, *swapped, *inits))
    distant, swapped, inits = got[:sides], got[sides : 4 * sides], got[4 * sides :]
    near = []
    for index, (part, init) in enumerate(zip(coeffs, inits)):
        near += [part, *swapped[3 * index : 3 * index + 3], init]

    coeff, seed, ahead = call(
        plan,
        weight_kernel,
        3,
        [(7, plan.layers, width, lanes), box, box],
        [(sides, 4, *piece), box],
        coeff_own,
        initial_own,
        *near,
    )
    fields, given = call(
        plan,
        field_kernel,
        0.5,
        [(plan.pairs, *box), (plan.pairs, plan.layers, plan.width_of(plan.mid), lanes)],
        [],
        guess_own,
        *beside,
        *distant,
    )
    keep, give = call(
        plan, total_kernel, 15, [(plan.side, far, lanes), (plan.side, far, lanes)], [box] * 3, coeff, ahead, fields
    )
    parts = call(
        plan,
        part_kernel,
        0.3,
        [(plan.side, plan.width_of(reach), lanes) for reach in plan.reach],
        [],
        keep,
        plan.send(give, flip=True),
    )
    mine = [plan.send(part, dz=distance) for distance, part in enumerate(parts, 1)]
    terms, begun = call(
        plan,
        term_kernel,
        15,
        [(plan.pairs, plan.layers, plan.chunk, lanes), (plan.layers, band, lanes)],
        [box] * 3,
        coeff,
        fields,
        plan.send(given, flip=True),
        seed,
    )
    (share,) = call(plan, start_kernel, 6, [(plan.layers, band, lanes)], [box] * 2, coeff, begun, *mine)
    results = call(
        plan,
        end_kernel,
        3,
        [(depth, plan.chunk, lanes)] * (1 + len(plan.others)),
        [box] * 2,
        coeff,
        share,
        plan.send(share, flip=True),
        terms,
    )
    back = [results[0]]
    for (dy, ds), part in zip(plan.others, results[1:]):
        back.append(plan.send(part, dy, ds))
    (out,) = call(
        plan, place_kernel, 1, [(depth, plan.rows, lanes)], [], *back, copies=len(back), out_whole=True
    )
    return out[None]


def padded_2(cells, sides, width):
    for axis, dim in sides:
        count = lax.axis_size(axis)
        ends = count - 1
        head = lax.slice_in_dim(cells, 0, width, axis=dim)
        tail = lax.slice_in_dim(cells, cells.shape[dim] - width, cells.shape[dim], axis=dim)
        cells = jnp.concatenate(
            [
                lax.ppermute(tail, axis, [(i, (i + 1) % count) for i in range(ends)]),
                cells,
                lax.ppermute(head, axis, [((i + 1) % count, i) for i in range(ends)]),
            ],
            axis=dim,
        )
    return cells


def from_behind(value, axis, steps):
    count = lax.axis_size(axis)
    first, last = (max(0, -steps), min(count, count - steps))
    return lax.ppermute(value, axis, [(source, source + steps) for source in range(first, last)])


def stencil(extended, diffus, pos_vel, neg_vel, diff_rate, adv_rate):
    center = extended[..., 1:-1, :, :]
    z_low = extended[..., :-2, :, :]
    z_high = extended[..., 2:, :, :]
    widths = [(0, 0)] * (center.ndim - 2) + [(1, 1), (1, 1)]
    padded = jnp.pad(center, widths)
    x_low = padded[..., :-2, 1:-1]
    x_high = padded[..., 2:, 1:-1]
    y_low = padded[..., 1:-1, :-2]
    y_high = padded[..., 1:-1, 2:]
    laplace = z_low + z_high + (x_low + x_high) + (y_low + y_high) - 6.0 * center
    advect = pos_vel[0] * (center - z_low) + neg_vel[0] * (z_high - center)
    advect = advect + pos_vel[1] * (center - x_low) + neg_vel[1] * (x_high - center)
    advect = advect + pos_vel[2] * (center - y_low) + neg_vel[2] * (y_high - center)
    return center + diff_rate * diffus * laplace - adv_rate * advect


def by_slabs(initial, guess, diffusivity, velocity):
    pos_vel = jnp.maximum(velocity, 0.0)
    neg_vel = jnp.minimum(velocity, 0.0)
    depth = diffusivity.shape[0]
    total_depth = depth * lax.axis_size("space")
    first_row = lax.axis_index("space") * depth
    block_index = lax.axis_index("tm")
    block_count = lax.axis_size("tm")
    state = guess[0]
    stacked = jnp.concatenate([diffusivity[None], velocity], axis=0)
    wide_coeff = padded_2(stacked, (("space", 1),), STEPS)
    wide_diff = wide_coeff[0]
    wide_pos = jnp.maximum(wide_coeff[1:], 0.0)
    wide_neg = jnp.minimum(wide_coeff[1:], 0.0)
    previous_end = from_behind(state, "tm", 1)
    starts = jnp.where(block_index == 0, initial, previous_end)
    current = padded_2(starts, (("space", 0),), STEPS)
    for step_index in range(STEPS):
        margin = STEPS - step_index - 1
        rows = depth + 2 * margin
        lower = step_index + 1
        fresh = stencil(
            current,
            wide_diff[lower : lower + rows],
            wide_pos[:, lower : lower + rows],
            wide_neg[:, lower : lower + rows],
            FINE_DIFF,
            FINE_ADV,
        )
        global_rows = first_row - margin + lax.iota(jnp.int32, rows)
        inside = (global_rows >= 0) & (global_rows < total_depth)
        current = jnp.where(inside[:, None, None], fresh, 0.0)
    residue = current - state

    def sweep_turn(index, carry):
        previous = from_behind(carry, "tm", 1)
        beside_all = padded_2(previous, (("space", 0),), 1)
        return stencil(beside_all, diffusivity, pos_vel, neg_vel, RATIO * FINE_DIFF, RATIO * FINE_ADV) + residue

    correction = lax.fori_loop(0, block_count, sweep_turn, jnp.zeros_like(state))
    state = state + correction
    return state[None]


def fits(plan):
    if plan.n_t % (2 * GROUP) or plan.layers % 2 or plan.rows % (plan.pairs * plan.n_s * TILE) or plan.lanes != LANES:
        return False
    return plan.n_s > 1 and 4 * 24 * plan.layers * plan.width * plan.lanes <= VMEM_BYTES


def per_device(initial, guess, diffusivity, velocity):
    shape, n_t, n_s = diffusivity.shape, lax.axis_size("tm"), lax.axis_size("space")
    way = by_regions if n_t > GROUP and fits(Plan(shape, n_t, n_s)) else by_slabs
    return way(initial, guess, diffusivity, velocity)


def solution(mesh):
    in_specs = (
        P("space", None, None),
        P("tm", "space", None, None),
        P("space", None, None),
        P(None, "space", None, None),
    )
    out_specs = P("tm", "space", None, None)
    return jax.shard_map(per_device, mesh=mesh, in_specs=in_specs, out_specs=out_specs, check_vma=False)
```

```python
import functools
import itertools
import math

import jax
import jax.numpy as jnp
from jax import lax
from jax.experimental import pallas as pl
from jax.experimental.pallas import tpu as pltpu
from jax.sharding import PartitionSpec as P

STEPS = 10
FINE_DIFF = 0.01
FINE_ADV = 0.012
RATIO = 10.0
GROUP = 4
TILE = 8
LANES = 128
SETS = 6
SPARE_BYTES = 4 * 1024 * 1024
VMEM_BYTES = 56 * 1024 * 1024
VMEM = pl.BlockSpec(memory_space=pltpu.VMEM)
HBM = pl.BlockSpec(memory_space=pltpu.HBM)


def rounded(count):
    return -(-count // TILE) * TILE


class Plan:
    def __init__(self, shape, n_t, n_s):
        self.n_t, self.n_s = n_t, n_s
        self.depth, self.rows, self.lanes = shape
        self.layers = self.depth * n_s
        self.pairs = GROUP // 2
        self.groups = n_t // GROUP
        self.chunk = self.rows // (self.pairs * n_s)
        self.halo = rounded(STEPS + n_t - 2)
        self.width = self.width_of(self.halo)
        self.wide = min(self.rows, self.width + 2 * TILE)
        self.reach = [GROUP * d - 1 for d in range(1, self.groups)]
        self.far = self.reach[-1]
        self.side = self.layers // 2
        self.others = [(dy, ds) for ds in range(n_s) for dy in range(self.pairs) if dy or ds]
        spans = [(y * n_s * self.chunk, (y + 1) * n_s * self.chunk) for y in range(self.pairs)]
        self.span = max(min(self.rows, end + self.halo) - max(0, start - self.halo) for start, end in spans)
        self.mid = STEPS + GROUP - 1

    def width_of(self, halo):
        return min(self.rows, self.chunk + 2 * rounded(halo))

    def start_of(self, chip, halo):
        start = jnp.clip(chip * self.chunk - rounded(halo), 0, self.rows - self.width_of(halo))
        return pl.multiple_of(start, TILE)

    def wide_start(self, chip):
        start = jnp.clip(chip * self.chunk - self.halo - TILE, 0, self.rows - self.wide)
        return pl.multiple_of(start, TILE)

    def reach_rows(self, distance):
        return min(self.rows, self.chunk + 2 * self.trim(distance))

    def trim(self, distance):
        return -(-self.reach[distance - 1] // 4) * 4

    def reach_start(self, chip, distance):
        start = jnp.clip(chip * self.chunk - self.trim(distance), 0, self.rows - self.reach_rows(distance))
        return pl.multiple_of(start, 4)

    def span_start(self, y):
        start = jnp.clip(y * self.n_s * self.chunk - self.halo, 0, self.rows - self.span)
        return pl.multiple_of(start, TILE)

    def box(self):
        return (self.layers + 2, self.width + 2 * TILE, self.lanes)

    def send(self, value, dy=0, ds=0, dz=0, flip=False, swap=False, first=False):
        pairs = []
        for t, s in itertools.product(range(self.n_t), range(self.n_s)):
            core, y, z = t % 2, (t // 2) % self.pairs, t // GROUP
            to_z = z ^ 1 if swap else 0 if first else z + dz
            if to_z >= self.groups or (first and (z < self.groups - 1 or core)):
                continue
            to_t = to_z * GROUP + (y + dy) % self.pairs * 2 + (core ^ int(flip))
            pairs.append((t * self.n_s + s, to_t * self.n_s + (s + ds) % self.n_s))
        return lax.ppermute(value, ("tm", "space"), pairs)


class Place:
    def __init__(self, plan):
        self.plan = plan
        t = lax.axis_index("tm")
        self.s = lax.axis_index("space")
        self.core = lax.rem(t, 2)
        self.y = lax.rem(lax.div(t, 2), plan.pairs)
        self.z = lax.div(t, GROUP)
        self.chip = self.y * plan.n_s + self.s
        self.base = plan.start_of(self.chip, plan.halo)

    def ahead(self, dy, ds):
        plan = self.plan
        return lax.rem(self.y + dy, plan.pairs) * plan.n_s + lax.rem(self.s + ds, plan.n_s)

    def behind(self, dy, ds):
        plan = self.plan
        return lax.rem(self.y + plan.pairs - dy, plan.pairs), lax.rem(self.s + plan.n_s - ds, plan.n_s)

    def inner(self, halo):
        return pl.multiple_of(self.plan.start_of(self.chip, halo) - self.base, TILE)


def fetch(sem, copies):
    started = [pltpu.make_async_copy(source, target, sem.at[index]) for index, (source, target) in enumerate(copies)]
    for copy in started:
        copy.start()
    return started


def shifts(lanes):
    row = lax.broadcasted_iota(jnp.int32, (2 * lanes, 2 * lanes), 0)
    row = jnp.where(row >= lanes, row - lanes, row)
    column = lax.broadcasted_iota(jnp.int32, (2 * lanes, 2 * lanes), 1)
    up = jnp.where(row == column - 1, 1.0, 0.0)
    down = jnp.where(row == column - lanes + 1, 1.0, 0.0)
    return jnp.where(column < lanes, up, down).astype(jnp.bfloat16)


def with_shifts(plan, body):
    count = plan.layers // 2

    def run(*sums):
        matrix = shifts(plan.lanes)
        for unit in range(2):
            pltpu.matmul_push_rhs(matrix, 0, unit)
            pltpu.matmul_acc_lhs(sums[unit], jnp.zeros((2 * TILE, 2 * plan.lanes), jnp.bfloat16), load_staged_rhs=0)
            pltpu.matmul_pop(sums[unit])
        body([sums[i * count : (i + 1) * count] for i in range(SETS)])

    pl.run_scoped(
        run,
        *[pltpu.ACC(i % count % 2)((2 * TILE, 2 * plan.lanes), jnp.float32) for i in range(SETS * count)],
    )


def stepper(plan, place, coeff, sums):
    count = plan.layers // 2

    def step(source, target, halo, scale, plus=None, minus=None):
        first = place.inner(halo)
        strips = plan.width_of(halo) // TILE

        def rows(index):
            return pl.multiple_of(first + index * TILE, TILE)

        def shift(index, which, pair):
            here = pl.ds(pl.multiple_of(rows(index) + TILE, TILE), TILE)
            value = source[pl.ds(1 + 2 * pair, 2), here, :].reshape(2 * TILE, plan.lanes)
            high = value.astype(jnp.bfloat16)
            rest = (value - high.astype(jnp.float32)).astype(jnp.bfloat16)
            pltpu.matmul_acc_lhs(sums[which][pair], jnp.concatenate([high, rest], axis=1))

        def strip(index, which, later, later_set):
            row = rows(index)
            inner = pl.ds(row, TILE)
            here = pl.ds(pl.multiple_of(row + TILE, TILE), TILE)
            low, mid = source[0, here, :], source[1, here, :]
            for layer in range(plan.layers):
                if layer % 2 == 0:
                    moved = pltpu.matmul_pop(sums[which][layer // 2])
                    shift(later, later_set, layer // 2)
                part = moved[layer % 2 * TILE : (layer % 2 + 1) * TILE]
                high = source[layer + 2, here, :]
                x_low = source[layer + 1, pl.ds(row + TILE - 1, TILE), :]
                x_high = source[layer + 1, pl.ds(row + TILE + 1, TILE), :]
                change = (coeff[0, layer, inner, :] * mid + coeff[1, layer, inner, :] * low) + (
                    coeff[2, layer, inner, :] * high + coeff[3, layer, inner, :] * x_low
                )
                change = change + (coeff[4, layer, inner, :] * x_high + coeff[5, layer, inner, :] * part[:, : plan.lanes])
                change = change + coeff[6, layer, inner, :] * part[:, plan.lanes :]
                fresh = mid + change if scale == 1.0 else mid + scale * change
                if plus is not None:
                    fresh = fresh + plus(layer, row)
                if minus is not None:
                    fresh = fresh - minus(layer, row)
                target[layer + 1, here, :] = fresh
                low, mid = mid, high

        sets = next(k for k in range(SETS, 1, -1) if strips % k == 0 or k == 2)
        ahead = sets - 1

        def bounded(index):
            return jnp.minimum(index, strips - 1)

        for index in range(ahead):
            for pair in range(count):
                shift(bounded(index), index, pair)

        def some(index, _):
            for which in range(sets):
                strip(
                    bounded(index * sets + which), which, bounded(index * sets + which + ahead), (which + ahead) % sets
                )
            return 0

        lax.fori_loop(0, -(-strips // sets), some, 0)
        for index in range(ahead):
            for pair in range(count):
                pltpu.matmul_pop(sums[index][pair])

    return step


def field_at(field):
    return lambda layer, row: field[layer + 1, pl.ds(pl.multiple_of(row + TILE, TILE), TILE), :]


def fine(step, source, one, two, halo, minus=None):
    now, turn = source, (one, two)
    for index in range(STEPS):
        last = index == STEPS - 1
        step(now, turn[index % 2], halo - 1 - index, 1.0, minus=minus if last else None)
        now = turn[index % 2]
    return now


def clear(plan, *fields):
    for field in fields:
        edge = jnp.zeros((TILE, plan.lanes), jnp.float32)
        for layer in range(plan.layers + 2):
            field[layer, :TILE, :] = edge
            field[layer, TILE + plan.width :, :] = edge
        for layer in (0, plan.layers + 1):
            field[layer] = jnp.zeros_like(field[layer])


def first_cut_kernel(plan, guess, initial, diff, vel, *refs):
    place = Place(plan)
    sem = refs[-1]
    coeffs, inits, blocks = refs[: plan.n_s - 1], refs[plan.n_s - 1 : 2 * plan.n_s - 2], refs[2 * plan.n_s - 2 : -1]
    which = place.core * 2 + lax.rem(place.z, 2)

    def source(ds, array):
        rows = pl.ds(plan.start_of(place.ahead(0, ds), plan.halo), plan.width)
        return diff.at[:, rows, :] if array is None else vel.at[array, :, rows, :]

    for ds, target in enumerate(coeffs, 1):

        @pl.when(which == 0)
        def _(ds=ds, target=target):
            pltpu.make_async_copy(source(ds, None), target, sem.at[ds - 1]).start()

        @pl.when(which > 0)
        def _(ds=ds, target=target):
            pltpu.make_async_copy(source(ds, jnp.maximum(which - 1, 0)), target, sem.at[ds - 1]).start()

    copies = []
    for dy, target in enumerate(blocks, 1):
        start = plan.span_start(lax.rem(place.y + dy, plan.pairs))
        copies.append(pltpu.make_async_copy(guess.at[0, :, pl.ds(start, plan.span), :], target, sem.at[2 * plan.n_s - 3 + dy]))
    for ds, target in enumerate(inits, 1):
        start = plan.wide_start(place.ahead(0, ds))
        source_rows = initial.at[:, pl.ds(start, plan.wide), :]
        copies.append(pltpu.make_async_copy(source_rows, target, sem.at[plan.n_s - 2 + ds]))
    for copy in copies:
        copy.start()
    for ds, target in enumerate(coeffs, 1):
        pltpu.make_async_copy(source(ds, None), target, sem.at[ds - 1]).wait()
    for copy in copies:
        copy.wait()


def second_cut_kernel(plan, guess, *refs):
    place = Place(plan)
    blocks, sem = refs[:-1], refs[-1]
    copies = []
    for ds, target in enumerate(blocks, 1):
        start = plan.start_of(place.ahead(0, ds), plan.halo)
        copies.append((guess.at[0, :, pl.ds(start, plan.width), :], target))
    for copy in fetch(sem, copies):
        copy.wait()


def own_cut_kernel(plan, guess, initial, diff, vel, guess_own, initial_own, coeff_own, sem):
    place = Place(plan)
    rows = pl.ds(place.base, plan.width)
    copies = [
        (guess.at[0, :, rows, :], guess_own),
        (initial.at[:, pl.ds(plan.wide_start(place.chip), plan.wide), :], initial_own),
        (diff.at[:, rows, :], coeff_own.at[0]),
        (vel.at[:, :, rows, :], coeff_own.at[pl.ds(1, 3)]),
    ]
    for copy in fetch(sem, copies):
        copy.wait()


def mix_kernel(plan, *refs):
    place = Place(plan)
    count = plan.n_s - 1
    own, others, outs = refs[:count], refs[count:-count], refs[-count:]
    for ds, (block, out) in enumerate(zip(own, outs), 1):
        out[0] = block[...]
        start = plan.start_of(place.ahead(0, ds), plan.halo) - plan.span_start(place.y)
        for slot, other in enumerate(others, 1):
            out[slot] = other[:, pl.ds(pl.multiple_of(start, TILE), plan.width), :]


def field_kernel(plan, own, *refs):
    place = Place(plan)
    beside, far = refs[: plan.pairs - 1], refs[plan.pairs - 1 : -2]
    fields, given = refs[-2:]
    clear(plan, *[fields.at[slot] for slot in range(plan.pairs)])
    rows = pl.ds(TILE, plan.width)
    given_rows = pl.ds(place.inner(plan.mid), plan.width_of(plan.mid))

    def take(dy, ds, read):
        slot, slab = place.behind(dy, ds)

        def layer(index, _):
            value = read(index)
            fields[slot, 1 + slab * plan.depth + index, rows, :] = value
            return 0

        lax.fori_loop(0, plan.depth, layer, 0)

    take(0, 0, lambda index: own[index])
    start = pl.multiple_of(place.base - plan.span_start(place.y), TILE)
    for dy, block in enumerate(beside, 1):
        take(dy, 0, lambda index, block=block: block[index, pl.ds(start, plan.width), :])
    for ds, blocks in enumerate(far, 1):
        for dy in range(plan.pairs):
            take(dy, ds, lambda index, blocks=blocks, dy=dy: blocks[dy, index])
    for slot in range(plan.pairs):
        for layer in range(plan.layers):
            given[slot, layer] = fields[slot, 1 + layer, pl.ds(pl.multiple_of(given_rows.start + TILE, TILE), given_rows.size), :]


def weight_kernel(plan, coeff_own, window, *refs):
    refs = list(refs)
    near, init_near = [], []
    for _ in range(plan.n_s - 1):
        near.append(refs[:4])
        init_near.append(refs[4])
        del refs[:5]
    coeff, seed, ahead, parts, one = refs
    place = Place(plan)
    z, core, s = place.z, place.core, place.s
    even = lax.rem(z, 2)
    for ds, (mine, swapped, flipped, both) in enumerate(near, 1):
        for ref, array in (
            (mine, 2 * core + even),
            (swapped, 2 * core + 1 - even),
            (flipped, 2 * (1 - core) + even),
            (both, 2 * (1 - core) + 1 - even),
        ):
            parts[ds - 1, array] = ref[...]
    lane = lax.broadcasted_iota(jnp.int32, (plan.width, plan.lanes), 1)
    for ds in range(plan.n_s):
        slab = place.behind(0, ds)[1]

        def layer_weights(layer, _, ds=ds, slab=slab):
            index = slab * plan.depth + layer
            held = parts.at[ds - 1] if ds else coeff_own
            spread = FINE_DIFF * held[0, layer]
            total = 6.0 * spread
            for k in range(3):
                drift = FINE_ADV * held[1 + k, layer]
                total = total + jnp.abs(drift)
                below = spread + jnp.maximum(drift, 0.0)
                above = spread - jnp.minimum(drift, 0.0)
                if k == 2:
                    below = jnp.where(lane == 0, 0.0, below)
                    above = jnp.where(lane == plan.lanes - 1, 0.0, above)
                coeff[1 + 2 * k, index] = below
                coeff[2 + 2 * k, index] = above
            coeff[0, index] = -total
            return 0

        lax.fori_loop(0, plan.depth, layer_weights, 0)

    @pl.when((z == 0) & (core == 0))
    def _():
        seed[...] = jnp.zeros_like(seed)
        offset = lax.div(place.base - plan.wide_start(place.chip), TILE) - 1

        def fill(target_layer, source):
            for index in range(plan.width // TILE + 2):
                strip = index + offset
                inside = (strip >= 0) & (strip < plan.wide // TILE)
                held = pl.ds(pl.multiple_of(jnp.clip(strip, 0, plan.wide // TILE - 1) * TILE, TILE), TILE)
                value = jnp.where(inside, source[held, :], 0.0)
                seed[target_layer, index * TILE : (index + 1) * TILE, :] = value

        for ds in range(plan.n_s):
            slab = place.behind(0, ds)[1]
            held = init_near[ds - 1] if ds else window

            def take(layer, _, held=held, slab=slab):
                fill(1 + slab * plan.depth + layer, held.at[layer])
                return 0

            lax.fori_loop(0, plan.depth, take, 0)

        def body(sums):
            step = stepper(plan, place, coeff, sums)
            clear(plan, ahead, one)
            now, turn, reach = seed, (ahead, one), STEPS + plan.n_t - 1
            for index in range(GROUP - 1):
                reach -= 1
                step(now, turn[index % 2], reach, RATIO)
                now = turn[index % 2]
            if now is one:
                ahead[...] = one[...]

        with_shifts(plan, body)


def total_kernel(plan, coeff, ahead, fields, keep, give, one, two, three):
    place = Place(plan)
    z, core = place.z, place.core
    clear(plan, one, two, three)

    def body(sums):
        step = stepper(plan, place, coeff, sums)
        reach = STEPS + plan.n_t - 2
        now = fields.at[0]
        for slot in range(1, plan.pairs):
            reach -= 1
            step(now, two, reach, RATIO)
            now, spare = two, (one if slot % 2 else three)
            reach -= 1
            step(now, spare, reach, RATIO, plus=field_at(fields.at[slot]))
            now = spare
        free = [f for f in (one, two, three) if f is not now]
        coarse = free.pop()
        step(now, coarse, reach - 1, RATIO)

        @pl.when((z == 0) & (core == 0))
        def _():
            for layer in range(1, plan.layers + 1):
                now[layer] = now[layer] + ahead[layer]

        share = fine(step, now, free[0], now, reach, minus=field_at(coarse))
        reach -= STEPS
        total = free[0]

        @pl.when(core == 0)
        def _():
            step(share, total, reach - 1, RATIO)

        @pl.when(core != 0)
        def _():
            for layer in range(1, plan.layers + 1):
                total[layer] = share[layer]

        inner = pl.ds(pl.multiple_of(place.inner(plan.far) + TILE, TILE), plan.width_of(plan.far))
        for layer in range(plan.side):
            keep[layer] = total[1 + core * plan.side + layer, inner, :]
            give[layer] = total[1 + (1 - core) * plan.side + layer, inner, :]

    with_shifts(plan, body)


def part_kernel(plan, keep, got, *outs):
    place = Place(plan)
    for distance, out in enumerate(outs, 1):
        start = plan.reach_start(place.chip, distance) - plan.start_of(place.chip, plan.far)
        rows = pl.ds(start, plan.reach_rows(distance))
        for layer in range(plan.side):
            out[layer] = keep[layer, rows, :] + got[layer, rows, :]


def term_kernel(plan, coeff, fields, flipped, seed, terms, begun, one, two, three):
    place = Place(plan)
    core = place.core
    clear(plan, one, two, three)
    middle = pl.ds(pl.multiple_of(place.inner(plan.mid) + TILE, TILE), plan.width_of(plan.mid))

    def body(sums):
        step = stepper(plan, place, coeff, sums)

        def term(source, coarse, other, reach, out, halo):
            step(source, coarse, reach - 1, RATIO)
            result = fine(step, source, other, source, reach, minus=field_at(coarse))
            rows = pl.ds(pl.multiple_of(place.inner(halo) + TILE, TILE), plan.width_of(halo))
            for layer in range(plan.layers):
                out[layer] = result[layer + 1, rows, :]

        def load(block, target):
            @pl.when(core == block % 2)
            def _():
                target[...] = fields[block // 2]

            @pl.when(core != block % 2)
            def _():
                for layer in range(plan.layers):
                    target[layer + 1, middle, :] = flipped[block // 2, layer]

        def block_term(block):
            load(0, one)
            left = STEPS + block - 1
            now, spare = one, two
            for before in range(1, block):
                load(before, three)
                left -= 1
                step(now, spare, left, RATIO, plus=field_at(three))
                now, spare = spare, now
            term(now, three, spare, left, terms.at[block // 2], 0)

        for block in range(GROUP):

            @pl.when(core == block % 2)
            def _(block=block):
                if block == 0:
                    terms[0] = jnp.zeros_like(terms[0])
                else:
                    block_term(block)

        started = (place.z == 0) & (core == 0)

        @pl.when(started)
        def _():
            one[...] = seed[...]
            result = fine(step, one, two, one, STEPS + GROUP - 1)
            rows = pl.ds(pl.multiple_of(place.inner(TILE) + TILE, TILE), plan.width_of(TILE))
            for layer in range(plan.layers):
                begun[layer] = result[layer + 1, rows, :]

        @pl.when(jnp.logical_not(started))
        def _():
            begun[...] = jnp.zeros_like(begun)

    with_shifts(plan, body)


def start_kernel(plan, coeff, begun, *refs):
    *totals, out, one, two = refs
    place = Place(plan)
    clear(plan, one, two)

    def body(sums):
        step = stepper(plan, place, coeff, sums)
        now, spare = one, two
        now[...] = jnp.zeros_like(now)
        for distance in range(len(totals), 0, -1):

            @pl.when(place.z >= distance)
            def _(distance=distance):
                reach = plan.reach[distance - 1]
                start = plan.reach_start(place.chip, distance) - place.base + TILE
                rows = pl.ds(start, plan.reach_rows(distance))
                for layer in range(plan.side):
                    index = 1 + place.core * plan.side + layer
                    now[index, rows, :] = now[index, rows, :] + totals[distance - 1][layer]
                if distance > 1:
                    for turn in range(GROUP):
                        source, target = (now, spare) if turn % 2 == 0 else (spare, now)
                        step(source, target, reach - 1 - turn, RATIO)

        rows = pl.ds(pl.multiple_of(place.inner(TILE) + TILE, TILE), plan.width_of(TILE))
        for layer in range(plan.layers):
            out[layer] = now[layer + 1, rows, :] + begun[layer]

    with_shifts(plan, body)


def end_kernel(plan, coeff, share, other, terms, *refs):
    *outs, one, two = refs
    place = Place(plan)
    core, s, y = place.core, place.s, place.y
    clear(plan, one, two)
    chunk = pl.ds(pl.multiple_of(place.inner(0) + TILE, TILE), plan.chunk)
    rows = pl.ds(pl.multiple_of(place.inner(TILE) + TILE, TILE), plan.width_of(TILE))
    for layer in range(plan.layers):
        one[layer + 1, rows, :] = share[layer] + other[layer]

    def write(block, field):
        @pl.when(core == block % 2)
        def _():
            for out, (dy, ds) in zip(outs, [(0, 0), *plan.others]):

                @pl.when(lax.rem(y + dy, plan.pairs) == block // 2)
                def _(out=out, ds=ds):
                    slab = lax.rem(s + ds, plan.n_s)
                    for layer in range(plan.depth):
                        value = field[1 + slab * plan.depth + layer, chunk, :]
                        out[layer] = value + terms[block // 2, slab * plan.depth + layer] if block else value

    def body(sums):
        step = stepper(plan, place, coeff, sums)
        now, spare = one, two
        write(0, now)
        for block in range(1, GROUP):
            step(now, spare, GROUP - 1 - block, RATIO)
            now, spare = spare, now
            write(block, now)

    with_shifts(plan, body)


def place_kernel(plan, *refs):
    place = Place(plan)
    out, sem, pieces = refs[-2], refs[-1], refs[:-2]
    copies = []
    for (dy, ds), piece in zip([(0, 0), *plan.others], pieces):
        y, s = place.behind(dy, ds)
        rows = pl.ds(pl.multiple_of((y * plan.n_s + s) * plan.chunk, TILE), plan.chunk)
        copies.append((piece, out.at[:, rows, :]))
    for copy in fetch(sem, copies):
        copy.wait()


def call(plan, kernel, micros, outs, scratch, *args, copies=0, whole=0, out_whole=False):
    spaces = [pltpu.HBM] * whole + [pltpu.VMEM] * (len(args) - whole)
    args = [pltpu.with_memory_space_constraint(arg, space) for arg, space in zip(args, spaces)]
    held = pltpu.HBM if out_whole else pltpu.VMEM
    needed = sum(4 * math.prod(shape) for shape in scratch)
    return pl.pallas_call(
        functools.partial(kernel, plan),
        out_shape=[held(shape, jnp.float32) for shape in outs],
        in_specs=[HBM] * whole + [VMEM] * (len(args) - whole),
        out_specs=[HBM if out_whole else VMEM] * len(outs),
        scratch_shapes=[pltpu.VMEM(shape, jnp.float32) for shape in scratch]
        + ([pltpu.SemaphoreType.DMA((copies,))] if copies else []),
        compiler_params=pltpu.CompilerParams(vmem_limit_bytes=needed + SPARE_BYTES),
        cost_estimate=pl.CostEstimate(flops=0, transcendentals=0, bytes_accessed=int(micros * 3.6e6)),
        name=kernel.__name__,
    )(*args)


def by_regions(initial, guess, diffusivity, velocity):
    plan = Plan(diffusivity.shape, lax.axis_size("tm"), lax.axis_size("space"))
    depth, lanes, width = plan.depth, plan.lanes, plan.width
    box, sides = plan.box(), plan.n_s - 1
    band, far = plan.width_of(TILE), plan.width_of(plan.far)
    window, piece = (depth, plan.wide, lanes), (depth, width, lanes)

    cuts = call(
        plan,
        first_cut_kernel,
        2,
        [piece] * sides + [window] * sides + [(depth, plan.span, lanes)] * (plan.pairs - 1),
        [],
        guess,
        initial,
        diffusivity,
        velocity,
        copies=2 * sides + plan.pairs - 1,
        whole=4,
    )
    got = [plan.send(part, ds=ds) for ds, part in enumerate(cuts[:sides], 1)]
    got += [plan.send(part, ds=ds, first=True) for ds, part in enumerate(cuts[sides : 2 * sides], 1)]
    got += [plan.send(part, dy=dy) for dy, part in enumerate(cuts[2 * sides :], 1)]
    own_sent = call(plan, second_cut_kernel, 1, [piece] * sides, [], guess, copies=sides, whole=1)
    guess_own, initial_own, coeff_own = call(
        plan, own_cut_kernel, 60, [piece, window, (4, *piece)], [], guess, initial, diffusivity, velocity, copies=4, whole=4
    )
    coeffs, inits, beside = got[:sides], got[sides : 2 * sides], got[2 * sides :]
    got = lax.optimization_barrier((*coeffs, *beside, *own_sent))
    coeffs, beside, own_sent = got[:sides], got[sides:-sides], got[-sides:]
    mixed = call(plan, mix_kernel, 0.3, [(plan.pairs, *piece)] * sides, [], *own_sent, *beside)
    distant = [plan.send(part, ds=ds) for ds, part in enumerate(mixed, 1)]
    swapped = []
    for part in coeffs:
        flipped, part = plan.send(part, flip=True), plan.send(part, swap=True)
        swapped += [part, flipped, plan.send(part, flip=True)]
    near = []
    for index, (part, init) in enumerate(zip(coeffs, inits)):
        near += [part, *swapped[3 * index : 3 * index + 3], init]

    coeff, seed, ahead = call(
        plan,
        weight_kernel,
        3,
        [(7, plan.layers, width, lanes), box, box],
        [(sides, 4, *piece), box],
        coeff_own,
        initial_own,
        *near,
    )
    coeff, *distant = lax.optimization_barrier((coeff, *distant))
    fields, given = call(
        plan,
        field_kernel,
        0.5,
        [(plan.pairs, *box), (plan.pairs, plan.layers, plan.width_of(plan.mid), lanes)],
        [],
        guess_own,
        *beside,
        *distant,
    )
    keep, give = call(
        plan, total_kernel, 15, [(plan.side, far, lanes), (plan.side, far, lanes)], [box] * 3, coeff, ahead, fields
    )
    parts = call(
        plan,
        part_kernel,
        0.3,
        [(plan.side, plan.reach_rows(distance), lanes) for distance in range(1, plan.groups)],
        [],
        keep,
        plan.send(give, flip=True),
    )
    mine = [plan.send(part, dz=distance) for distance, part in enumerate(parts, 1)]
    terms, begun = call(
        plan,
        term_kernel,
        15,
        [(plan.pairs, plan.layers, plan.chunk, lanes), (plan.layers, band, lanes)],
        [box] * 3,
        coeff,
        fields,
        plan.send(given, flip=True),
        seed,
    )
    (share,) = call(plan, start_kernel, 6, [(plan.layers, band, lanes)], [box] * 2, coeff, begun, *mine)
    results = call(
        plan,
        end_kernel,
        3,
        [(depth, plan.chunk, lanes)] * (1 + len(plan.others)),
        [box] * 2,
        coeff,
        share,
        plan.send(share, flip=True),
        terms,
    )
    back = [results[0]]
    for (dy, ds), part in zip(plan.others, results[1:]):
        back.append(plan.send(part, dy, ds))
    (out,) = call(
        plan, place_kernel, 1, [(depth, plan.rows, lanes)], [], *back, copies=len(back), out_whole=True
    )
    return out[None]


def padded_2(cells, sides, width):
    for axis, dim in sides:
        count = lax.axis_size(axis)
        ends = count - 1
        head = lax.slice_in_dim(cells, 0, width, axis=dim)
        tail = lax.slice_in_dim(cells, cells.shape[dim] - width, cells.shape[dim], axis=dim)
        cells = jnp.concatenate(
            [
                lax.ppermute(tail, axis, [(i, (i + 1) % count) for i in range(ends)]),
                cells,
                lax.ppermute(head, axis, [((i + 1) % count, i) for i in range(ends)]),
            ],
            axis=dim,
        )
    return cells


def from_behind(value, axis, steps):
    count = lax.axis_size(axis)
    first, last = (max(0, -steps), min(count, count - steps))
    return lax.ppermute(value, axis, [(source, source + steps) for source in range(first, last)])


def stencil(extended, diffus, pos_vel, neg_vel, diff_rate, adv_rate):
    center = extended[..., 1:-1, :, :]
    z_low = extended[..., :-2, :, :]
    z_high = extended[..., 2:, :, :]
    widths = [(0, 0)] * (center.ndim - 2) + [(1, 1), (1, 1)]
    padded = jnp.pad(center, widths)
    x_low = padded[..., :-2, 1:-1]
    x_high = padded[..., 2:, 1:-1]
    y_low = padded[..., 1:-1, :-2]
    y_high = padded[..., 1:-1, 2:]
    laplace = z_low + z_high + (x_low + x_high) + (y_low + y_high) - 6.0 * center
    advect = pos_vel[0] * (center - z_low) + neg_vel[0] * (z_high - center)
    advect = advect + pos_vel[1] * (center - x_low) + neg_vel[1] * (x_high - center)
    advect = advect + pos_vel[2] * (center - y_low) + neg_vel[2] * (y_high - center)
    return center + diff_rate * diffus * laplace - adv_rate * advect


def by_slabs(initial, guess, diffusivity, velocity):
    pos_vel = jnp.maximum(velocity, 0.0)
    neg_vel = jnp.minimum(velocity, 0.0)
    depth = diffusivity.shape[0]
    total_depth = depth * lax.axis_size("space")
    first_row = lax.axis_index("space") * depth
    block_index = lax.axis_index("tm")
    block_count = lax.axis_size("tm")
    state = guess[0]
    stacked = jnp.concatenate([diffusivity[None], velocity], axis=0)
    wide_coeff = padded_2(stacked, (("space", 1),), STEPS)
    wide_diff = wide_coeff[0]
    wide_pos = jnp.maximum(wide_coeff[1:], 0.0)
    wide_neg = jnp.minimum(wide_coeff[1:], 0.0)
    previous_end = from_behind(state, "tm", 1)
    starts = jnp.where(block_index == 0, initial, previous_end)
    current = padded_2(starts, (("space", 0),), STEPS)
    for step_index in range(STEPS):
        margin = STEPS - step_index - 1
        rows = depth + 2 * margin
        lower = step_index + 1
        fresh = stencil(
            current,
            wide_diff[lower : lower + rows],
            wide_pos[:, lower : lower + rows],
            wide_neg[:, lower : lower + rows],
            FINE_DIFF,
            FINE_ADV,
        )
        global_rows = first_row - margin + lax.iota(jnp.int32, rows)
        inside = (global_rows >= 0) & (global_rows < total_depth)
        current = jnp.where(inside[:, None, None], fresh, 0.0)
    residue = current - state

    def sweep_turn(index, carry):
        previous = from_behind(carry, "tm", 1)
        beside_all = padded_2(previous, (("space", 0),), 1)
        return stencil(beside_all, diffusivity, pos_vel, neg_vel, RATIO * FINE_DIFF, RATIO * FINE_ADV) + residue

    correction = lax.fori_loop(0, block_count, sweep_turn, jnp.zeros_like(state))
    state = state + correction
    return state[None]


def fits(plan):
    if plan.n_t % (2 * GROUP) or plan.layers % 2 or plan.rows % (plan.pairs * plan.n_s * TILE) or plan.lanes != LANES:
        return False
    return plan.n_s > 1 and 4 * 24 * plan.layers * plan.width * plan.lanes <= VMEM_BYTES


def per_device(initial, guess, diffusivity, velocity):
    shape, n_t, n_s = diffusivity.shape, lax.axis_size("tm"), lax.axis_size("space")
    way = by_regions if n_t > GROUP and fits(Plan(shape, n_t, n_s)) else by_slabs
    return way(initial, guess, diffusivity, velocity)


def solution(mesh):
    in_specs = (
        P("space", None, None),
        P("tm", "space", None, None),
        P("space", None, None),
        P(None, "space", None, None),
    )
    out_specs = P("tm", "space", None, None)
    return jax.shard_map(per_device, mesh=mesh, in_specs=in_specs, out_specs=out_specs, check_vma=False)
```

```python
import functools
import itertools
import math

import jax
import jax.numpy as jnp
from jax import lax
from jax.experimental import pallas as pl
from jax.experimental.pallas import tpu as pltpu
from jax.sharding import PartitionSpec as P

STEPS = 10
FINE_DIFF = 0.01
FINE_ADV = 0.012
RATIO = 10.0
GROUP = 4
TILE = 8
LANES = 128
SETS = 6
SPARE_BYTES = 4 * 1024 * 1024
VMEM_BYTES = 56 * 1024 * 1024
VMEM = pl.BlockSpec(memory_space=pltpu.VMEM)
HBM = pl.BlockSpec(memory_space=pltpu.HBM)


def rounded(count):
    return -(-count // TILE) * TILE


class Plan:
    def __init__(self, shape, n_t, n_s):
        self.n_t, self.n_s = n_t, n_s
        self.depth, self.rows, self.lanes = shape
        self.layers = self.depth * n_s
        self.pairs = GROUP // 2
        self.groups = n_t // GROUP
        self.chunk = self.rows // (self.pairs * n_s)
        self.halo = rounded(STEPS + n_t - 2)
        self.width = self.width_of(self.halo)
        self.wide = min(self.rows, self.width + 2 * TILE)
        self.reach = [GROUP * d - 1 for d in range(1, self.groups)]
        self.far = self.reach[-1]
        self.side = self.layers // 2
        self.others = [(dy, ds) for ds in range(n_s) for dy in range(self.pairs) if dy or ds]
        spans = [(y * n_s * self.chunk, (y + 1) * n_s * self.chunk) for y in range(self.pairs)]
        self.span = max(min(self.rows, end + self.halo) - max(0, start - self.halo) for start, end in spans)
        self.mid = STEPS + GROUP - 1

    def width_of(self, halo):
        return min(self.rows, self.chunk + 2 * rounded(halo))

    def start_of(self, chip, halo):
        start = jnp.clip(chip * self.chunk - rounded(halo), 0, self.rows - self.width_of(halo))
        return pl.multiple_of(start, TILE)

    def wide_start(self, chip):
        start = jnp.clip(chip * self.chunk - self.halo - TILE, 0, self.rows - self.wide)
        return pl.multiple_of(start, TILE)

    def reach_rows(self, distance):
        return min(self.rows, self.chunk + 2 * self.trim(distance))

    def trim(self, distance):
        return -(-self.reach[distance - 1] // 4) * 4

    def reach_start(self, chip, distance):
        start = jnp.clip(chip * self.chunk - self.trim(distance), 0, self.rows - self.reach_rows(distance))
        return pl.multiple_of(start, 4)

    def span_start(self, y):
        start = jnp.clip(y * self.n_s * self.chunk - self.halo, 0, self.rows - self.span)
        return pl.multiple_of(start, TILE)

    def box(self):
        return (self.layers + 2, self.width + 2 * TILE, self.lanes)

    def send(self, value, dy=0, ds=0, dz=0, flip=False, swap=False, first=False):
        pairs = []
        for t, s in itertools.product(range(self.n_t), range(self.n_s)):
            core, y, z = t % 2, (t // 2) % self.pairs, t // GROUP
            to_z = z ^ 1 if swap else 0 if first else z + dz
            if to_z >= self.groups or (first and (z < self.groups - 1 or core)):
                continue
            to_t = to_z * GROUP + (y + dy) % self.pairs * 2 + (core ^ int(flip))
            pairs.append((t * self.n_s + s, to_t * self.n_s + (s + ds) % self.n_s))
        return lax.ppermute(value, ("tm", "space"), pairs)


class Place:
    def __init__(self, plan):
        self.plan = plan
        t = lax.axis_index("tm")
        self.s = lax.axis_index("space")
        self.core = lax.rem(t, 2)
        self.y = lax.rem(lax.div(t, 2), plan.pairs)
        self.z = lax.div(t, GROUP)
        self.chip = self.y * plan.n_s + self.s
        self.base = plan.start_of(self.chip, plan.halo)

    def ahead(self, dy, ds):
        plan = self.plan
        return lax.rem(self.y + dy, plan.pairs) * plan.n_s + lax.rem(self.s + ds, plan.n_s)

    def behind(self, dy, ds):
        plan = self.plan
        return lax.rem(self.y + plan.pairs - dy, plan.pairs), lax.rem(self.s + plan.n_s - ds, plan.n_s)

    def inner(self, halo):
        return pl.multiple_of(self.plan.start_of(self.chip, halo) - self.base, TILE)


def fetch(sem, copies):
    started = [pltpu.make_async_copy(source, target, sem.at[index]) for index, (source, target) in enumerate(copies)]
    for copy in started:
        copy.start()
    return started


def shifts(lanes):
    row = lax.broadcasted_iota(jnp.int32, (2 * lanes, 2 * lanes), 0)
    row = jnp.where(row >= lanes, row - lanes, row)
    column = lax.broadcasted_iota(jnp.int32, (2 * lanes, 2 * lanes), 1)
    up = jnp.where(row == column - 1, 1.0, 0.0)
    down = jnp.where(row == column - lanes + 1, 1.0, 0.0)
    return jnp.where(column < lanes, up, down).astype(jnp.bfloat16)


def with_shifts(plan, body):
    count = plan.layers // 2

    def run(*sums):
        matrix = shifts(plan.lanes)
        for unit in range(2):
            pltpu.matmul_push_rhs(matrix, 0, unit)
            pltpu.matmul_acc_lhs(sums[unit], jnp.zeros((2 * TILE, 2 * plan.lanes), jnp.bfloat16), load_staged_rhs=0)
            pltpu.matmul_pop(sums[unit])
        body([sums[i * count : (i + 1) * count] for i in range(SETS)])

    pl.run_scoped(
        run,
        *[pltpu.ACC(i % count % 2)((2 * TILE, 2 * plan.lanes), jnp.float32) for i in range(SETS * count)],
    )


def stepper(plan, place, coeff, sums):
    count = plan.layers // 2

    def step(source, target, halo, scale, plus=None, minus=None):
        first = place.inner(halo)
        strips = plan.width_of(halo) // TILE

        def rows(index):
            return pl.multiple_of(first + index * TILE, TILE)

        def shift(index, which, pair):
            here = pl.ds(pl.multiple_of(rows(index) + TILE, TILE), TILE)
            value = source[pl.ds(1 + 2 * pair, 2), here, :].reshape(2 * TILE, plan.lanes)
            high = value.astype(jnp.bfloat16)
            rest = (value - high.astype(jnp.float32)).astype(jnp.bfloat16)
            pltpu.matmul_acc_lhs(sums[which][pair], jnp.concatenate([high, rest], axis=1))

        def strip(index, which, later, later_set):
            row = rows(index)
            inner = pl.ds(row, TILE)
            here = pl.ds(pl.multiple_of(row + TILE, TILE), TILE)
            low, mid = source[0, here, :], source[1, here, :]
            for layer in range(plan.layers):
                if layer % 2 == 0:
                    moved = pltpu.matmul_pop(sums[which][layer // 2])
                    if later is not None:
                        shift(later, later_set, layer // 2)
                part = moved[layer % 2 * TILE : (layer % 2 + 1) * TILE]
                high = source[layer + 2, here, :]
                x_low = source[layer + 1, pl.ds(row + TILE - 1, TILE), :]
                x_high = source[layer + 1, pl.ds(row + TILE + 1, TILE), :]
                change = (coeff[0, layer, inner, :] * mid + coeff[1, layer, inner, :] * low) + (
                    coeff[2, layer, inner, :] * high + coeff[3, layer, inner, :] * x_low
                )
                change = change + (coeff[4, layer, inner, :] * x_high + coeff[5, layer, inner, :] * part[:, : plan.lanes])
                change = change + coeff[6, layer, inner, :] * part[:, plan.lanes :]
                fresh = mid + change if scale == 1.0 else mid + scale * change
                if plus is not None:
                    fresh = fresh + plus(layer, row)
                if minus is not None:
                    fresh = fresh - minus(layer, row)
                target[layer + 1, here, :] = fresh
                low, mid = mid, high

        ahead = min(SETS - 1, strips)
        for index in range(ahead):
            for pair in range(count):
                shift(index, index, pair)
        for index in range(strips):
            strip(index, index % SETS, index + ahead if index + ahead < strips else None, (index + ahead) % SETS)

    return step


def field_at(field):
    return lambda layer, row: field[layer + 1, pl.ds(pl.multiple_of(row + TILE, TILE), TILE), :]


def repeat(step, now, spare, halos, scale):
    for _, same in itertools.groupby(halos, key=rounded):
        same = list(same)

        def twice(_, carry, halo=same[0], now=now, spare=spare):
            step(now, spare, halo, scale)
            step(spare, now, halo, scale)
            return carry

        if len(same) > 1:
            lax.fori_loop(0, len(same) // 2, twice, 0)
        if len(same) % 2:
            step(now, spare, same[-1], scale)
            now, spare = spare, now
    return now, spare


def fine(step, source, one, two, halo, minus=None):
    step(source, one, halo - 1, 1.0)
    now, spare = repeat(step, one, two, range(halo - 2, halo - STEPS, -1), 1.0)
    step(now, spare, halo - STEPS, 1.0, minus=minus)
    return spare


def clear(plan, *fields):
    for field in fields:
        edge = jnp.zeros((TILE, plan.lanes), jnp.float32)
        for layer in range(plan.layers + 2):
            field[layer, :TILE, :] = edge
            field[layer, TILE + plan.width :, :] = edge
        for layer in (0, plan.layers + 1):
            field[layer] = jnp.zeros_like(field[layer])


def first_cut_kernel(plan, guess, initial, diff, vel, *refs):
    place = Place(plan)
    sem = refs[-1]
    coeffs, inits, blocks = refs[: plan.n_s - 1], refs[plan.n_s - 1 : 2 * plan.n_s - 2], refs[2 * plan.n_s - 2 : -1]
    which = place.core * 2 + lax.rem(place.z, 2)

    def source(ds, array):
        rows = pl.ds(plan.start_of(place.ahead(0, ds), plan.halo), plan.width)
        return diff.at[:, rows, :] if array is None else vel.at[array, :, rows, :]

    for ds, target in enumerate(coeffs, 1):

        @pl.when(which == 0)
        def _(ds=ds, target=target):
            pltpu.make_async_copy(source(ds, None), target, sem.at[ds - 1]).start()

        @pl.when(which > 0)
        def _(ds=ds, target=target):
            pltpu.make_async_copy(source(ds, jnp.maximum(which - 1, 0)), target, sem.at[ds - 1]).start()

    copies = []
    for dy, target in enumerate(blocks, 1):
        start = plan.span_start(lax.rem(place.y + dy, plan.pairs))
        copies.append(pltpu.make_async_copy(guess.at[0, :, pl.ds(start, plan.span), :], target, sem.at[2 * plan.n_s - 3 + dy]))
    for ds, target in enumerate(inits, 1):
        start = plan.wide_start(place.ahead(0, ds))
        source_rows = initial.at[:, pl.ds(start, plan.wide), :]
        copies.append(pltpu.make_async_copy(source_rows, target, sem.at[plan.n_s - 2 + ds]))
    for copy in copies:
        copy.start()
    for ds, target in enumerate(coeffs, 1):
        pltpu.make_async_copy(source(ds, None), target, sem.at[ds - 1]).wait()
    for copy in copies:
        copy.wait()


def second_cut_kernel(plan, guess, *refs):
    place = Place(plan)
    blocks, sem = refs[:-1], refs[-1]
    copies = []
    for ds, target in enumerate(blocks, 1):
        start = plan.start_of(place.ahead(0, ds), plan.halo)
        copies.append((guess.at[0, :, pl.ds(start, plan.width), :], target))
    for copy in fetch(sem, copies):
        copy.wait()


def own_cut_kernel(plan, guess, initial, diff, vel, guess_own, initial_own, coeff_own, sem):
    place = Place(plan)
    rows = pl.ds(place.base, plan.width)
    copies = [
        (guess.at[0, :, rows, :], guess_own),
        (initial.at[:, pl.ds(plan.wide_start(place.chip), plan.wide), :], initial_own),
        (diff.at[:, rows, :], coeff_own.at[0]),
        (vel.at[:, :, rows, :], coeff_own.at[pl.ds(1, 3)]),
    ]
    for copy in fetch(sem, copies):
        copy.wait()


def mix_kernel(plan, *refs):
    place = Place(plan)
    count = plan.n_s - 1
    own, others, outs = refs[:count], refs[count:-count], refs[-count:]
    for ds, (block, out) in enumerate(zip(own, outs), 1):
        out[0] = block[...]
        start = plan.start_of(place.ahead(0, ds), plan.halo) - plan.span_start(place.y)
        for slot, other in enumerate(others, 1):
            out[slot] = other[:, pl.ds(pl.multiple_of(start, TILE), plan.width), :]


def field_kernel(plan, own, *refs):
    place = Place(plan)
    beside, far = refs[: plan.pairs - 1], refs[plan.pairs - 1 : -2]
    fields, given = refs[-2:]
    clear(plan, *[fields.at[slot] for slot in range(plan.pairs)])
    rows = pl.ds(TILE, plan.width)
    given_rows = pl.ds(place.inner(plan.mid), plan.width_of(plan.mid))

    def take(dy, ds, read):
        slot, slab = place.behind(dy, ds)

        def layer(index, _):
            value = read(index)
            fields[slot, 1 + slab * plan.depth + index, rows, :] = value
            return 0

        lax.fori_loop(0, plan.depth, layer, 0)

    take(0, 0, lambda index: own[index])
    start = pl.multiple_of(place.base - plan.span_start(place.y), TILE)
    for dy, block in enumerate(beside, 1):
        take(dy, 0, lambda index, block=block: block[index, pl.ds(start, plan.width), :])
    for ds, blocks in enumerate(far, 1):
        for dy in range(plan.pairs):
            take(dy, ds, lambda index, blocks=blocks, dy=dy: blocks[dy, index])
    for slot in range(plan.pairs):
        for layer in range(plan.layers):
            given[slot, layer] = fields[slot, 1 + layer, pl.ds(pl.multiple_of(given_rows.start + TILE, TILE), given_rows.size), :]


def weight_kernel(plan, coeff_own, window, *refs):
    refs = list(refs)
    near, init_near = [], []
    for _ in range(plan.n_s - 1):
        near.append(refs[:4])
        init_near.append(refs[4])
        del refs[:5]
    coeff, seed, ahead, parts, one = refs
    place = Place(plan)
    z, core, s = place.z, place.core, place.s
    even = lax.rem(z, 2)
    for ds, (mine, swapped, flipped, both) in enumerate(near, 1):
        for ref, array in (
            (mine, 2 * core + even),
            (swapped, 2 * core + 1 - even),
            (flipped, 2 * (1 - core) + even),
            (both, 2 * (1 - core) + 1 - even),
        ):
            parts[ds - 1, array] = ref[...]
    lane = lax.broadcasted_iota(jnp.int32, (plan.width, plan.lanes), 1)
    for ds in range(plan.n_s):
        slab = place.behind(0, ds)[1]

        def layer_weights(layer, _, ds=ds, slab=slab):
            index = slab * plan.depth + layer
            held = parts.at[ds - 1] if ds else coeff_own
            spread = FINE_DIFF * held[0, layer]
            total = 6.0 * spread
            for k in range(3):
                drift = FINE_ADV * held[1 + k, layer]
                total = total + jnp.abs(drift)
                below = spread + jnp.maximum(drift, 0.0)
                above = spread - jnp.minimum(drift, 0.0)
                if k == 2:
                    below = jnp.where(lane == 0, 0.0, below)
                    above = jnp.where(lane == plan.lanes - 1, 0.0, above)
                coeff[1 + 2 * k, index] = below
                coeff[2 + 2 * k, index] = above
            coeff[0, index] = -total
            return 0

        lax.fori_loop(0, plan.depth, layer_weights, 0)

    @pl.when((z == 0) & (core == 0))
    def _():
        seed[...] = jnp.zeros_like(seed)
        offset = lax.div(place.base - plan.wide_start(place.chip), TILE) - 1

        def fill(target_layer, source):
            for index in range(plan.width // TILE + 2):
                strip = index + offset
                inside = (strip >= 0) & (strip < plan.wide // TILE)
                held = pl.ds(pl.multiple_of(jnp.clip(strip, 0, plan.wide // TILE - 1) * TILE, TILE), TILE)
                value = jnp.where(inside, source[held, :], 0.0)
                seed[target_layer, index * TILE : (index + 1) * TILE, :] = value

        for ds in range(plan.n_s):
            slab = place.behind(0, ds)[1]
            held = init_near[ds - 1] if ds else window

            def take(layer, _, held=held, slab=slab):
                fill(1 + slab * plan.depth + layer, held.at[layer])
                return 0

            lax.fori_loop(0, plan.depth, take, 0)

        def body(sums):
            step = stepper(plan, place, coeff, sums)
            clear(plan, ahead, one)
            reach = STEPS + plan.n_t - 2
            step(seed, ahead, reach, RATIO)
            now, _ = repeat(step, ahead, one, range(reach - 1, reach - GROUP + 1, -1), RATIO)
            if now is one:
                ahead[...] = one[...]

        with_shifts(plan, body)


def total_kernel(plan, coeff, ahead, fields, keep, give, one, two, three):
    place = Place(plan)
    z, core = place.z, place.core
    clear(plan, one, two, three)

    def body(sums):
        step = stepper(plan, place, coeff, sums)
        reach = STEPS + plan.n_t - 2
        now = fields.at[0]
        for slot in range(1, plan.pairs):
            reach -= 1
            step(now, two, reach, RATIO)
            now, spare = two, (one if slot % 2 else three)
            reach -= 1
            step(now, spare, reach, RATIO, plus=field_at(fields.at[slot]))
            now = spare
        free = [f for f in (one, two, three) if f is not now]
        coarse = free.pop()
        step(now, coarse, reach - 1, RATIO)

        @pl.when((z == 0) & (core == 0))
        def _():
            for layer in range(1, plan.layers + 1):
                now[layer] = now[layer] + ahead[layer]

        share = fine(step, now, free[0], now, reach, minus=field_at(coarse))
        reach -= STEPS
        total = free[0]

        @pl.when(core == 0)
        def _():
            step(share, total, reach - 1, RATIO)

        @pl.when(core != 0)
        def _():
            for layer in range(1, plan.layers + 1):
                total[layer] = share[layer]

        inner = pl.ds(pl.multiple_of(place.inner(plan.far) + TILE, TILE), plan.width_of(plan.far))
        for layer in range(plan.side):
            keep[layer] = total[1 + core * plan.side + layer, inner, :]
            give[layer] = total[1 + (1 - core) * plan.side + layer, inner, :]

    with_shifts(plan, body)


def part_kernel(plan, keep, got, *outs):
    place = Place(plan)
    for distance, out in enumerate(outs, 1):
        start = plan.reach_start(place.chip, distance) - plan.start_of(place.chip, plan.far)
        rows = pl.ds(start, plan.reach_rows(distance))
        for layer in range(plan.side):
            out[layer] = keep[layer, rows, :] + got[layer, rows, :]


def term_kernel(plan, coeff, fields, flipped, seed, terms, begun, one, two, three):
    place = Place(plan)
    core = place.core
    clear(plan, one, two, three)
    middle = pl.ds(pl.multiple_of(place.inner(plan.mid) + TILE, TILE), plan.width_of(plan.mid))
    chunk = pl.ds(pl.multiple_of(place.inner(0) + TILE, TILE), plan.chunk)

    def body(sums):
        step = stepper(plan, place, coeff, sums)

        def load(block, target):
            @pl.when(core == block % 2)
            def _():
                target[...] = fields[block // 2]

            @pl.when(core != block % 2)
            def _():
                for layer in range(plan.layers):
                    target[layer + 1, middle, :] = flipped[block // 2, layer]

        def slot_terms(slot, _):
            last = 2 * slot + core
            load(0, one)
            for before in range(1, GROUP - 1):

                @pl.when(before < last)
                def _(before=before):
                    load(before, three)
                    step(one, two, STEPS + GROUP - 2 - before, RATIO, plus=field_at(three))
                    one[...] = two[...]

            @pl.when(last > 0)
            def _():
                step(one, three, STEPS - 1, RATIO)
                result = fine(step, one, two, one, STEPS, minus=field_at(three))
                for layer in range(plan.layers):
                    terms[slot, layer] = result[layer + 1, chunk, :]

            @pl.when(last == 0)
            def _():
                terms[0] = jnp.zeros_like(terms[0])

            return 0

        lax.fori_loop(0, plan.pairs, slot_terms, 0)

        started = (place.z == 0) & (core == 0)

        @pl.when(started)
        def _():
            one[...] = seed[...]
            result = fine(step, one, two, one, STEPS + GROUP - 1)
            rows = pl.ds(pl.multiple_of(place.inner(TILE) + TILE, TILE), plan.width_of(TILE))
            for layer in range(plan.layers):
                begun[layer] = result[layer + 1, rows, :]

        @pl.when(jnp.logical_not(started))
        def _():
            begun[...] = jnp.zeros_like(begun)

    with_shifts(plan, body)


def start_kernel(plan, coeff, begun, *refs):
    *totals, out, one, two = refs
    place = Place(plan)
    clear(plan, one, two)

    def body(sums):
        step = stepper(plan, place, coeff, sums)
        now, spare = one, two
        now[...] = jnp.zeros_like(now)
        for distance in range(len(totals), 0, -1):

            @pl.when(place.z >= distance)
            def _(distance=distance):
                reach = plan.reach[distance - 1]
                start = plan.reach_start(place.chip, distance) - place.base + TILE
                rows = pl.ds(start, plan.reach_rows(distance))
                for layer in range(plan.side):
                    index = 1 + place.core * plan.side + layer
                    now[index, rows, :] = now[index, rows, :] + totals[distance - 1][layer]
                if distance > 1:
                    repeat(step, now, spare, range(reach - 1, reach - 1 - GROUP, -1), RATIO)

        rows = pl.ds(pl.multiple_of(place.inner(TILE) + TILE, TILE), plan.width_of(TILE))
        for layer in range(plan.layers):
            out[layer] = now[layer + 1, rows, :] + begun[layer]

    with_shifts(plan, body)


def end_kernel(plan, coeff, share, other, terms, *refs):
    *outs, one, two = refs
    place = Place(plan)
    core, s, y = place.core, place.s, place.y
    clear(plan, one, two)
    chunk = pl.ds(pl.multiple_of(place.inner(0) + TILE, TILE), plan.chunk)
    rows = pl.ds(pl.multiple_of(place.inner(TILE) + TILE, TILE), plan.width_of(TILE))
    for layer in range(plan.layers):
        one[layer + 1, rows, :] = share[layer] + other[layer]

    def write(block, field):
        @pl.when(core == block % 2)
        def _():
            for out, (dy, ds) in zip(outs, [(0, 0), *plan.others]):

                @pl.when(lax.rem(y + dy, plan.pairs) == block // 2)
                def _(out=out, ds=ds):
                    slab = lax.rem(s + ds, plan.n_s)
                    for layer in range(plan.depth):
                        value = field[1 + slab * plan.depth + layer, chunk, :]
                        out[layer] = value + terms[block // 2, slab * plan.depth + layer] if block else value

    def body(sums):
        step = stepper(plan, place, coeff, sums)
        now, spare = one, two
        write(0, now)
        for block in range(1, GROUP):
            step(now, spare, GROUP - 1 - block, RATIO)
            now, spare = spare, now
            write(block, now)

    with_shifts(plan, body)


def place_kernel(plan, *refs):
    place = Place(plan)
    out, sem, pieces = refs[-2], refs[-1], refs[:-2]
    copies = []
    for (dy, ds), piece in zip([(0, 0), *plan.others], pieces):
        y, s = place.behind(dy, ds)
        rows = pl.ds(pl.multiple_of((y * plan.n_s + s) * plan.chunk, TILE), plan.chunk)
        copies.append((piece, out.at[:, rows, :]))
    for copy in fetch(sem, copies):
        copy.wait()


def call(plan, kernel, micros, outs, scratch, *args, copies=0, whole=0, out_whole=False):
    spaces = [pltpu.HBM] * whole + [pltpu.VMEM] * (len(args) - whole)
    args = [pltpu.with_memory_space_constraint(arg, space) for arg, space in zip(args, spaces)]
    held = pltpu.HBM if out_whole else pltpu.VMEM
    needed = sum(4 * math.prod(shape) for shape in scratch)
    return pl.pallas_call(
        functools.partial(kernel, plan),
        out_shape=[held(shape, jnp.float32) for shape in outs],
        in_specs=[HBM] * whole + [VMEM] * (len(args) - whole),
        out_specs=[HBM if out_whole else VMEM] * len(outs),
        scratch_shapes=[pltpu.VMEM(shape, jnp.float32) for shape in scratch]
        + ([pltpu.SemaphoreType.DMA((copies,))] if copies else []),
        compiler_params=pltpu.CompilerParams(vmem_limit_bytes=needed + SPARE_BYTES),
        cost_estimate=pl.CostEstimate(flops=0, transcendentals=0, bytes_accessed=int(micros * 3.6e6)),
        name=kernel.__name__,
    )(*args)


def by_regions(initial, guess, diffusivity, velocity):
    plan = Plan(diffusivity.shape, lax.axis_size("tm"), lax.axis_size("space"))
    depth, lanes, width = plan.depth, plan.lanes, plan.width
    box, sides = plan.box(), plan.n_s - 1
    band, far = plan.width_of(TILE), plan.width_of(plan.far)
    window, piece = (depth, plan.wide, lanes), (depth, width, lanes)

    cuts = call(
        plan,
        first_cut_kernel,
        2,
        [piece] * sides + [window] * sides + [(depth, plan.span, lanes)] * (plan.pairs - 1),
        [],
        guess,
        initial,
        diffusivity,
        velocity,
        copies=2 * sides + plan.pairs - 1,
        whole=4,
    )
    got = [plan.send(part, ds=ds) for ds, part in enumerate(cuts[:sides], 1)]
    got += [plan.send(part, ds=ds, first=True) for ds, part in enumerate(cuts[sides : 2 * sides], 1)]
    got += [plan.send(part, dy=dy) for dy, part in enumerate(cuts[2 * sides :], 1)]
    own_sent = call(plan, second_cut_kernel, 1, [piece] * sides, [], guess, copies=sides, whole=1)
    guess_own, initial_own, coeff_own = call(
        plan, own_cut_kernel, 60, [piece, window, (4, *piece)], [], guess, initial, diffusivity, velocity, copies=4, whole=4
    )
    coeffs, inits, beside = got[:sides], got[sides : 2 * sides], got[2 * sides :]
    got = lax.optimization_barrier((*coeffs, *own_sent, *beside))
    coeffs, own_sent, beside = got[:sides], got[sides : 2 * sides], got[2 * sides :]
    mixed = call(plan, mix_kernel, 0.3, [(plan.pairs, *piece)] * sides, [], *own_sent, *beside)
    distant = [plan.send(part, ds=ds) for ds, part in enumerate(mixed, 1)]
    swapped = []
    for part in coeffs:
        flipped, part = plan.send(part, flip=True), plan.send(part, swap=True)
        swapped += [part, flipped, plan.send(part, flip=True)]
    near = []
    for index, (part, init) in enumerate(zip(coeffs, inits)):
        near += [part, *swapped[3 * index : 3 * index + 3], init]

    coeff, seed, ahead = call(
        plan,
        weight_kernel,
        3,
        [(7, plan.layers, width, lanes), box, box],
        [(sides, 4, *piece), box],
        coeff_own,
        initial_own,
        *near,
    )
    coeff, *distant = lax.optimization_barrier((coeff, *distant))
    fields, given = call(
        plan,
        field_kernel,
        0.5,
        [(plan.pairs, *box), (plan.pairs, plan.layers, plan.width_of(plan.mid), lanes)],
        [],
        guess_own,
        *beside,
        *distant,
    )
    keep, give = call(
        plan, total_kernel, 15, [(plan.side, far, lanes), (plan.side, far, lanes)], [box] * 3, coeff, ahead, fields
    )
    parts = call(
        plan,
        part_kernel,
        0.3,
        [(plan.side, plan.reach_rows(distance), lanes) for distance in range(1, plan.groups)],
        [],
        keep,
        plan.send(give, flip=True),
    )
    mine = [plan.send(part, dz=distance) for distance, part in enumerate(parts, 1)]
    terms, begun = call(
        plan,
        term_kernel,
        15,
        [(plan.pairs, plan.layers, plan.chunk, lanes), (plan.layers, band, lanes)],
        [box] * 3,
        coeff,
        fields,
        plan.send(given, flip=True),
        seed,
    )
    (share,) = call(plan, start_kernel, 6, [(plan.layers, band, lanes)], [box] * 2, coeff, begun, *mine)
    results = call(
        plan,
        end_kernel,
        3,
        [(depth, plan.chunk, lanes)] * (1 + len(plan.others)),
        [box] * 2,
        coeff,
        share,
        plan.send(share, flip=True),
        terms,
    )
    back = [results[0]]
    for (dy, ds), part in zip(plan.others, results[1:]):
        back.append(plan.send(part, dy, ds))
    (out,) = call(
        plan, place_kernel, 1, [(depth, plan.rows, lanes)], [], *back, copies=len(back), out_whole=True
    )
    return out[None]


def padded_2(cells, sides, width):
    for axis, dim in sides:
        count = lax.axis_size(axis)
        ends = count - 1
        head = lax.slice_in_dim(cells, 0, width, axis=dim)
        tail = lax.slice_in_dim(cells, cells.shape[dim] - width, cells.shape[dim], axis=dim)
        cells = jnp.concatenate(
            [
                lax.ppermute(tail, axis, [(i, (i + 1) % count) for i in range(ends)]),
                cells,
                lax.ppermute(head, axis, [((i + 1) % count, i) for i in range(ends)]),
            ],
            axis=dim,
        )
    return cells


def from_behind(value, axis, steps):
    count = lax.axis_size(axis)
    first, last = (max(0, -steps), min(count, count - steps))
    return lax.ppermute(value, axis, [(source, source + steps) for source in range(first, last)])


def stencil(extended, diffus, pos_vel, neg_vel, diff_rate, adv_rate):
    center = extended[..., 1:-1, :, :]
    z_low = extended[..., :-2, :, :]
    z_high = extended[..., 2:, :, :]
    widths = [(0, 0)] * (center.ndim - 2) + [(1, 1), (1, 1)]
    padded = jnp.pad(center, widths)
    x_low = padded[..., :-2, 1:-1]
    x_high = padded[..., 2:, 1:-1]
    y_low = padded[..., 1:-1, :-2]
    y_high = padded[..., 1:-1, 2:]
    laplace = z_low + z_high + (x_low + x_high) + (y_low + y_high) - 6.0 * center
    advect = pos_vel[0] * (center - z_low) + neg_vel[0] * (z_high - center)
    advect = advect + pos_vel[1] * (center - x_low) + neg_vel[1] * (x_high - center)
    advect = advect + pos_vel[2] * (center - y_low) + neg_vel[2] * (y_high - center)
    return center + diff_rate * diffus * laplace - adv_rate * advect


def by_slabs(initial, guess, diffusivity, velocity):
    pos_vel = jnp.maximum(velocity, 0.0)
    neg_vel = jnp.minimum(velocity, 0.0)
    depth = diffusivity.shape[0]
    total_depth = depth * lax.axis_size("space")
    first_row = lax.axis_index("space") * depth
    block_index = lax.axis_index("tm")
    block_count = lax.axis_size("tm")
    state = guess[0]
    stacked = jnp.concatenate([diffusivity[None], velocity], axis=0)
    wide_coeff = padded_2(stacked, (("space", 1),), STEPS)
    wide_diff = wide_coeff[0]
    wide_pos = jnp.maximum(wide_coeff[1:], 0.0)
    wide_neg = jnp.minimum(wide_coeff[1:], 0.0)
    previous_end = from_behind(state, "tm", 1)
    starts = jnp.where(block_index == 0, initial, previous_end)
    current = padded_2(starts, (("space", 0),), STEPS)
    for step_index in range(STEPS):
        margin = STEPS - step_index - 1
        rows = depth + 2 * margin
        lower = step_index + 1
        fresh = stencil(
            current,
            wide_diff[lower : lower + rows],
            wide_pos[:, lower : lower + rows],
            wide_neg[:, lower : lower + rows],
            FINE_DIFF,
            FINE_ADV,
        )
        global_rows = first_row - margin + lax.iota(jnp.int32, rows)
        inside = (global_rows >= 0) & (global_rows < total_depth)
        current = jnp.where(inside[:, None, None], fresh, 0.0)
    residue = current - state

    def sweep_turn(index, carry):
        previous = from_behind(carry, "tm", 1)
        beside_all = padded_2(previous, (("space", 0),), 1)
        return stencil(beside_all, diffusivity, pos_vel, neg_vel, RATIO * FINE_DIFF, RATIO * FINE_ADV) + residue

    correction = lax.fori_loop(0, block_count, sweep_turn, jnp.zeros_like(state))
    state = state + correction
    return state[None]


def fits(plan):
    if plan.n_t % (2 * GROUP) or plan.layers % 2 or plan.rows % (plan.pairs * plan.n_s * TILE) or plan.lanes != LANES:
        return False
    return plan.n_s > 1 and 4 * 24 * plan.layers * plan.width * plan.lanes <= VMEM_BYTES


def per_device(initial, guess, diffusivity, velocity):
    shape, n_t, n_s = diffusivity.shape, lax.axis_size("tm"), lax.axis_size("space")
    way = by_regions if n_t > GROUP and fits(Plan(shape, n_t, n_s)) else by_slabs
    return way(initial, guess, diffusivity, velocity)


def solution(mesh):
    in_specs = (
        P("space", None, None),
        P("tm", "space", None, None),
        P("space", None, None),
        P(None, "space", None, None),
    )
    out_specs = P("tm", "space", None, None)
    return jax.shard_map(per_device, mesh=mesh, in_specs=in_specs, out_specs=out_specs, check_vma=False)
```

```python
import functools
import itertools
import math

import jax
import jax.numpy as jnp
from jax import lax
from jax.experimental import pallas as pl
from jax.experimental.pallas import tpu as pltpu
from jax.sharding import PartitionSpec as P

STEPS = 10
FINE_DIFF = 0.01
FINE_ADV = 0.012
RATIO = 10.0
GROUP = 4
TILE = 8
LANES = 128
SETS = 6
SPARE_BYTES = 4 * 1024 * 1024
VMEM_BYTES = 56 * 1024 * 1024
VMEM = pl.BlockSpec(memory_space=pltpu.VMEM)
HBM = pl.BlockSpec(memory_space=pltpu.HBM)


def rounded(count):
    return -(-count // TILE) * TILE


class Plan:
    def __init__(self, shape, n_t, n_s):
        self.n_t, self.n_s = n_t, n_s
        self.depth, self.rows, self.lanes = shape
        self.layers = self.depth * n_s
        self.pairs = GROUP // 2
        self.groups = n_t // GROUP
        self.chunk = self.rows // (self.pairs * n_s)
        self.halo = rounded(STEPS + n_t - 2)
        self.width = self.width_of(self.halo)
        self.wide = min(self.rows, self.width + 2 * TILE)
        self.reach = [GROUP * d - 1 for d in range(1, self.groups)]
        self.far = self.reach[-1]
        self.side = self.layers // 2
        self.others = [(dy, ds) for ds in range(n_s) for dy in range(self.pairs) if dy or ds]
        spans = [(y * n_s * self.chunk, (y + 1) * n_s * self.chunk) for y in range(self.pairs)]
        self.span = max(min(self.rows, end + self.halo) - max(0, start - self.halo) for start, end in spans)
        self.mid = STEPS + GROUP - 1

    def width_of(self, halo):
        return min(self.rows, self.chunk + 2 * rounded(halo))

    def start_of(self, chip, halo):
        start = jnp.clip(chip * self.chunk - rounded(halo), 0, self.rows - self.width_of(halo))
        return pl.multiple_of(start, TILE)

    def wide_start(self, chip):
        start = jnp.clip(chip * self.chunk - self.halo - TILE, 0, self.rows - self.wide)
        return pl.multiple_of(start, TILE)

    def reach_rows(self, distance):
        return min(self.rows, self.chunk + 2 * self.trim(distance))

    def trim(self, distance):
        return -(-self.reach[distance - 1] // 4) * 4

    def reach_start(self, chip, distance):
        start = jnp.clip(chip * self.chunk - self.trim(distance), 0, self.rows - self.reach_rows(distance))
        return pl.multiple_of(start, 4)

    def span_start(self, y):
        start = jnp.clip(y * self.n_s * self.chunk - self.halo, 0, self.rows - self.span)
        return pl.multiple_of(start, TILE)

    def box(self):
        return (self.layers + 2, self.width + 2 * TILE, self.lanes)

    def send(self, value, dy=0, ds=0, dz=0, flip=False, swap=False, first=False):
        pairs = []
        for t, s in itertools.product(range(self.n_t), range(self.n_s)):
            core, y, z = t % 2, (t // 2) % self.pairs, t // GROUP
            to_z = z ^ 1 if swap else 0 if first else z + dz
            if to_z >= self.groups or (first and (z < self.groups - 1 or core)):
                continue
            to_t = to_z * GROUP + (y + dy) % self.pairs * 2 + (core ^ int(flip))
            pairs.append((t * self.n_s + s, to_t * self.n_s + (s + ds) % self.n_s))
        return lax.ppermute(value, ("tm", "space"), pairs)


class Place:
    def __init__(self, plan):
        self.plan = plan
        t = lax.axis_index("tm")
        self.s = lax.axis_index("space")
        self.core = lax.rem(t, 2)
        self.y = lax.rem(lax.div(t, 2), plan.pairs)
        self.z = lax.div(t, GROUP)
        self.chip = self.y * plan.n_s + self.s
        self.base = plan.start_of(self.chip, plan.halo)

    def ahead(self, dy, ds):
        plan = self.plan
        return lax.rem(self.y + dy, plan.pairs) * plan.n_s + lax.rem(self.s + ds, plan.n_s)

    def behind(self, dy, ds):
        plan = self.plan
        return lax.rem(self.y + plan.pairs - dy, plan.pairs), lax.rem(self.s + plan.n_s - ds, plan.n_s)

    def inner(self, halo):
        return pl.multiple_of(self.plan.start_of(self.chip, halo) - self.base, TILE)


def fetch(sem, copies):
    started = [pltpu.make_async_copy(source, target, sem.at[index]) for index, (source, target) in enumerate(copies)]
    for copy in started:
        copy.start()
    return started


def shifts(lanes):
    row = lax.broadcasted_iota(jnp.int32, (2 * lanes, 2 * lanes), 0)
    row = jnp.where(row >= lanes, row - lanes, row)
    column = lax.broadcasted_iota(jnp.int32, (2 * lanes, 2 * lanes), 1)
    up = jnp.where(row == column - 1, 1.0, 0.0)
    down = jnp.where(row == column - lanes + 1, 1.0, 0.0)
    return jnp.where(column < lanes, up, down).astype(jnp.bfloat16)


def with_shifts(plan, body):
    count = plan.layers // 2

    def run(*sums):
        matrix = shifts(plan.lanes)
        for unit in range(2):
            pltpu.matmul_push_rhs(matrix, 0, unit)
            pltpu.matmul_acc_lhs(sums[unit], jnp.zeros((2 * TILE, 2 * plan.lanes), jnp.bfloat16), load_staged_rhs=0)
            pltpu.matmul_pop(sums[unit])
        body([sums[i * count : (i + 1) * count] for i in range(SETS)])

    pl.run_scoped(
        run,
        *[pltpu.ACC(i % count % 2)((2 * TILE, 2 * plan.lanes), jnp.float32) for i in range(SETS * count)],
    )


def stepper(plan, place, coeff, sums):
    count = plan.layers // 2

    def step(source, target, halo, scale, plus=None, minus=None):
        first = place.inner(halo)
        strips = plan.width_of(halo) // TILE
        own = 0 if scale == 1.0 else 7

        def rows(index):
            return pl.multiple_of(first + index * TILE, TILE)

        def shift(index, which, pair):
            here = pl.ds(pl.multiple_of(rows(index) + TILE, TILE), TILE)
            value = source[pl.ds(1 + 2 * pair, 2), here, :].reshape(2 * TILE, plan.lanes)
            high = value.astype(jnp.bfloat16)
            rest = (value - high.astype(jnp.float32)).astype(jnp.bfloat16)
            pltpu.matmul_acc_lhs(sums[which][pair], jnp.concatenate([high, rest], axis=1))

        def strip(index, which, later, later_set):
            row = rows(index)
            inner = pl.ds(row, TILE)
            here = pl.ds(pl.multiple_of(row + TILE, TILE), TILE)
            low, mid = source[0, here, :], source[1, here, :]
            for layer in range(plan.layers):
                if layer % 2 == 0:
                    moved = pltpu.matmul_pop(sums[which][layer // 2])
                    if later is not None:
                        shift(later, later_set, layer // 2)
                part = moved[layer % 2 * TILE : (layer % 2 + 1) * TILE]
                high = source[layer + 2, here, :]
                x_low = source[layer + 1, pl.ds(row + TILE - 1, TILE), :]
                x_high = source[layer + 1, pl.ds(row + TILE + 1, TILE), :]
                change = (coeff[own, layer, inner, :] * mid + coeff[1, layer, inner, :] * low) + (
                    coeff[2, layer, inner, :] * high + coeff[3, layer, inner, :] * x_low
                )
                change = change + (coeff[4, layer, inner, :] * x_high + coeff[5, layer, inner, :] * part[:, : plan.lanes])
                change = change + coeff[6, layer, inner, :] * part[:, plan.lanes :]
                fresh = change if scale == 1.0 else scale * change
                if plus is not None:
                    fresh = fresh + plus(layer, row)
                if minus is not None:
                    fresh = fresh - minus(layer, row)
                target[layer + 1, here, :] = fresh
                low, mid = mid, high

        ahead = min(SETS - 1, strips)
        for index in range(ahead):
            for pair in range(count):
                shift(index, index, pair)
        for index in range(strips):
            strip(index, index % SETS, index + ahead if index + ahead < strips else None, (index + ahead) % SETS)

    return step


def field_at(field):
    return lambda layer, row: field[layer + 1, pl.ds(pl.multiple_of(row + TILE, TILE), TILE), :]


def repeat(step, now, spare, halos, scale):
    for _, same in itertools.groupby(halos, key=rounded):
        same = list(same)

        def twice(_, carry, halo=same[0], now=now, spare=spare):
            step(now, spare, halo, scale)
            step(spare, now, halo, scale)
            return carry

        if len(same) > 1:
            lax.fori_loop(0, len(same) // 2, twice, 0)
        if len(same) % 2:
            step(now, spare, same[-1], scale)
            now, spare = spare, now
    return now, spare


def fine(step, source, one, two, halo, minus=None):
    step(source, one, halo - 1, 1.0)
    now, spare = repeat(step, one, two, range(halo - 2, halo - STEPS, -1), 1.0)
    step(now, spare, halo - STEPS, 1.0, minus=minus)
    return spare


def clear(plan, *fields):
    for field in fields:
        edge = jnp.zeros((TILE, plan.lanes), jnp.float32)
        for layer in range(plan.layers + 2):
            field[layer, :TILE, :] = edge
            field[layer, TILE + plan.width :, :] = edge
        for layer in (0, plan.layers + 1):
            field[layer] = jnp.zeros_like(field[layer])


def first_cut_kernel(plan, guess, initial, diff, vel, *refs):
    place = Place(plan)
    sem = refs[-1]
    coeffs, inits, blocks = refs[: plan.n_s - 1], refs[plan.n_s - 1 : 2 * plan.n_s - 2], refs[2 * plan.n_s - 2 : -1]
    which = place.core * 2 + lax.rem(place.z, 2)

    def source(ds, array):
        rows = pl.ds(plan.start_of(place.ahead(0, ds), plan.halo), plan.width)
        return diff.at[:, rows, :] if array is None else vel.at[array, :, rows, :]

    for ds, target in enumerate(coeffs, 1):

        @pl.when(which == 0)
        def _(ds=ds, target=target):
            pltpu.make_async_copy(source(ds, None), target, sem.at[ds - 1]).start()

        @pl.when(which > 0)
        def _(ds=ds, target=target):
            pltpu.make_async_copy(source(ds, jnp.maximum(which - 1, 0)), target, sem.at[ds - 1]).start()

    copies = []
    for dy, target in enumerate(blocks, 1):
        start = plan.span_start(lax.rem(place.y + dy, plan.pairs))
        copies.append(pltpu.make_async_copy(guess.at[0, :, pl.ds(start, plan.span), :], target, sem.at[2 * plan.n_s - 3 + dy]))
    for ds, target in enumerate(inits, 1):
        start = plan.wide_start(place.ahead(0, ds))
        source_rows = initial.at[:, pl.ds(start, plan.wide), :]
        copies.append(pltpu.make_async_copy(source_rows, target, sem.at[plan.n_s - 2 + ds]))
    for copy in copies:
        copy.start()
    for ds, target in enumerate(coeffs, 1):
        pltpu.make_async_copy(source(ds, None), target, sem.at[ds - 1]).wait()
    for copy in copies:
        copy.wait()


def second_cut_kernel(plan, guess, *refs):
    place = Place(plan)
    blocks, sem = refs[:-1], refs[-1]
    copies = []
    for ds, target in enumerate(blocks, 1):
        start = plan.start_of(place.ahead(0, ds), plan.halo)
        copies.append((guess.at[0, :, pl.ds(start, plan.width), :], target))
    for copy in fetch(sem, copies):
        copy.wait()


def own_cut_kernel(plan, guess, initial, diff, vel, guess_own, initial_own, coeff_own, sem):
    place = Place(plan)
    rows = pl.ds(place.base, plan.width)
    copies = [
        (guess.at[0, :, rows, :], guess_own),
        (initial.at[:, pl.ds(plan.wide_start(place.chip), plan.wide), :], initial_own),
        (diff.at[:, rows, :], coeff_own.at[0]),
        (vel.at[:, :, rows, :], coeff_own.at[pl.ds(1, 3)]),
    ]
    for copy in fetch(sem, copies):
        copy.wait()


def mix_kernel(plan, *refs):
    place = Place(plan)
    count = plan.n_s - 1
    own, others, outs = refs[:count], refs[count:-count], refs[-count:]
    for ds, (block, out) in enumerate(zip(own, outs), 1):
        out[0] = block[...]
        start = plan.start_of(place.ahead(0, ds), plan.halo) - plan.span_start(place.y)
        for slot, other in enumerate(others, 1):
            out[slot] = other[:, pl.ds(pl.multiple_of(start, TILE), plan.width), :]


def field_kernel(plan, own, *refs):
    place = Place(plan)
    beside, far = refs[: plan.pairs - 1], refs[plan.pairs - 1 : -2]
    fields, given = refs[-2:]
    clear(plan, *[fields.at[slot] for slot in range(plan.pairs)])
    rows = pl.ds(TILE, plan.width)
    given_rows = pl.ds(place.inner(plan.mid), plan.width_of(plan.mid))

    def take(dy, ds, read):
        slot, slab = place.behind(dy, ds)

        def layer(index, _):
            value = read(index)
            fields[slot, 1 + slab * plan.depth + index, rows, :] = value
            return 0

        lax.fori_loop(0, plan.depth, layer, 0)

    take(0, 0, lambda index: own[index])
    start = pl.multiple_of(place.base - plan.span_start(place.y), TILE)
    for dy, block in enumerate(beside, 1):
        take(dy, 0, lambda index, block=block: block[index, pl.ds(start, plan.width), :])
    for ds, blocks in enumerate(far, 1):
        for dy in range(plan.pairs):
            take(dy, ds, lambda index, blocks=blocks, dy=dy: blocks[dy, index])
    for slot in range(plan.pairs):
        for layer in range(plan.layers):
            given[slot, layer] = fields[slot, 1 + layer, pl.ds(pl.multiple_of(given_rows.start + TILE, TILE), given_rows.size), :]


def weight_kernel(plan, coeff_own, window, *refs):
    refs = list(refs)
    near, init_near = [], []
    for _ in range(plan.n_s - 1):
        near.append(refs[:4])
        init_near.append(refs[4])
        del refs[:5]
    coeff, seed, ahead, parts, one = refs
    place = Place(plan)
    z, core, s = place.z, place.core, place.s
    even = lax.rem(z, 2)
    for ds, (mine, swapped, flipped, both) in enumerate(near, 1):
        for ref, array in (
            (mine, 2 * core + even),
            (swapped, 2 * core + 1 - even),
            (flipped, 2 * (1 - core) + even),
            (both, 2 * (1 - core) + 1 - even),
        ):
            parts[ds - 1, array] = ref[...]
    lane = lax.broadcasted_iota(jnp.int32, (plan.width, plan.lanes), 1)
    for ds in range(plan.n_s):
        slab = place.behind(0, ds)[1]

        def layer_weights(layer, _, ds=ds, slab=slab):
            index = slab * plan.depth + layer
            held = parts.at[ds - 1] if ds else coeff_own
            spread = FINE_DIFF * held[0, layer]
            total = 6.0 * spread
            for k in range(3):
                drift = FINE_ADV * held[1 + k, layer]
                total = total + jnp.abs(drift)
                below = spread + jnp.maximum(drift, 0.0)
                above = spread - jnp.minimum(drift, 0.0)
                if k == 2:
                    below = jnp.where(lane == 0, 0.0, below)
                    above = jnp.where(lane == plan.lanes - 1, 0.0, above)
                coeff[1 + 2 * k, index] = below
                coeff[2 + 2 * k, index] = above
            coeff[0, index] = 1.0 - total
            coeff[7, index] = 1.0 / RATIO - total
            return 0

        lax.fori_loop(0, plan.depth, layer_weights, 0)

    @pl.when((z == 0) & (core == 0))
    def _():
        seed[...] = jnp.zeros_like(seed)
        offset = lax.div(place.base - plan.wide_start(place.chip), TILE) - 1

        def fill(target_layer, source):
            for index in range(plan.width // TILE + 2):
                strip = index + offset
                inside = (strip >= 0) & (strip < plan.wide // TILE)
                held = pl.ds(pl.multiple_of(jnp.clip(strip, 0, plan.wide // TILE - 1) * TILE, TILE), TILE)
                value = jnp.where(inside, source[held, :], 0.0)
                seed[target_layer, index * TILE : (index + 1) * TILE, :] = value

        for ds in range(plan.n_s):
            slab = place.behind(0, ds)[1]
            held = init_near[ds - 1] if ds else window

            def take(layer, _, held=held, slab=slab):
                fill(1 + slab * plan.depth + layer, held.at[layer])
                return 0

            lax.fori_loop(0, plan.depth, take, 0)

        def body(sums):
            step = stepper(plan, place, coeff, sums)
            clear(plan, ahead, one)
            reach = STEPS + plan.n_t - 2
            step(seed, ahead, reach, RATIO)
            now, _ = repeat(step, ahead, one, range(reach - 1, reach - GROUP + 1, -1), RATIO)
            if now is one:
                ahead[...] = one[...]

        with_shifts(plan, body)


def total_kernel(plan, coeff, ahead, fields, keep, give, one, two, three):
    place = Place(plan)
    z, core = place.z, place.core
    clear(plan, one, two, three)

    def body(sums):
        step = stepper(plan, place, coeff, sums)
        reach = STEPS + plan.n_t - 2
        now = fields.at[0]
        for slot in range(1, plan.pairs):
            reach -= 1
            step(now, two, reach, RATIO)
            now, spare = two, (one if slot % 2 else three)
            reach -= 1
            step(now, spare, reach, RATIO, plus=field_at(fields.at[slot]))
            now = spare
        free = [f for f in (one, two, three) if f is not now]
        coarse = free.pop()
        step(now, coarse, reach - 1, RATIO)

        @pl.when((z == 0) & (core == 0))
        def _():
            for layer in range(1, plan.layers + 1):
                now[layer] = now[layer] + ahead[layer]

        share = fine(step, now, free[0], now, reach, minus=field_at(coarse))
        reach -= STEPS
        total = free[0]

        @pl.when(core == 0)
        def _():
            step(share, total, reach - 1, RATIO)

        @pl.when(core != 0)
        def _():
            for layer in range(1, plan.layers + 1):
                total[layer] = share[layer]

        inner = pl.ds(pl.multiple_of(place.inner(plan.far) + TILE, TILE), plan.width_of(plan.far))
        for layer in range(plan.side):
            keep[layer] = total[1 + core * plan.side + layer, inner, :]
            give[layer] = total[1 + (1 - core) * plan.side + layer, inner, :]

    with_shifts(plan, body)


def part_kernel(plan, keep, got, *outs):
    place = Place(plan)
    for distance, out in enumerate(outs, 1):
        start = plan.reach_start(place.chip, distance) - plan.start_of(place.chip, plan.far)
        rows = pl.ds(start, plan.reach_rows(distance))
        for layer in range(plan.side):
            out[layer] = keep[layer, rows, :] + got[layer, rows, :]


def term_kernel(plan, coeff, fields, flipped, seed, terms, begun, one, two, three):
    place = Place(plan)
    core = place.core
    clear(plan, one, two, three)
    middle = pl.ds(pl.multiple_of(place.inner(plan.mid) + TILE, TILE), plan.width_of(plan.mid))
    chunk = pl.ds(pl.multiple_of(place.inner(0) + TILE, TILE), plan.chunk)

    def body(sums):
        step = stepper(plan, place, coeff, sums)

        def load(block, target):
            @pl.when(core == block % 2)
            def _():
                target[...] = fields[block // 2]

            @pl.when(core != block % 2)
            def _():
                for layer in range(plan.layers):
                    target[layer + 1, middle, :] = flipped[block // 2, layer]

        def slot_terms(slot, _):
            last = 2 * slot + core
            load(0, one)
            for before in range(1, GROUP - 1):

                @pl.when(before < last)
                def _(before=before):
                    load(before, three)
                    step(one, two, STEPS + GROUP - 2 - before, RATIO, plus=field_at(three))
                    one[...] = two[...]

            @pl.when(last > 0)
            def _():
                step(one, three, STEPS - 1, RATIO)
                result = fine(step, one, two, one, STEPS, minus=field_at(three))
                for layer in range(plan.layers):
                    terms[slot, layer] = result[layer + 1, chunk, :]

            @pl.when(last == 0)
            def _():
                terms[0] = jnp.zeros_like(terms[0])

            return 0

        lax.fori_loop(0, plan.pairs, slot_terms, 0)

        started = (place.z == 0) & (core == 0)

        @pl.when(started)
        def _():
            one[...] = seed[...]
            result = fine(step, one, two, one, STEPS + GROUP - 1)
            rows = pl.ds(pl.multiple_of(place.inner(TILE) + TILE, TILE), plan.width_of(TILE))
            for layer in range(plan.layers):
                begun[layer] = result[layer + 1, rows, :]

        @pl.when(jnp.logical_not(started))
        def _():
            begun[...] = jnp.zeros_like(begun)

    with_shifts(plan, body)


def start_kernel(plan, coeff, begun, *refs):
    *totals, out, one, two = refs
    totals = totals[::-1]
    place = Place(plan)
    clear(plan, one, two)

    def body(sums):
        step = stepper(plan, place, coeff, sums)
        now, spare = one, two
        now[...] = jnp.zeros_like(now)
        for distance in range(len(totals), 0, -1):

            @pl.when(place.z >= distance)
            def _(distance=distance):
                reach = plan.reach[distance - 1]
                start = plan.reach_start(place.chip, distance) - place.base + TILE
                rows = pl.ds(start, plan.reach_rows(distance))
                for layer in range(plan.side):
                    index = 1 + place.core * plan.side + layer
                    now[index, rows, :] = now[index, rows, :] + totals[distance - 1][layer]
                if distance > 1:
                    repeat(step, now, spare, range(reach - 1, reach - 1 - GROUP, -1), RATIO)

        rows = pl.ds(pl.multiple_of(place.inner(TILE) + TILE, TILE), plan.width_of(TILE))
        for layer in range(plan.layers):
            out[layer] = now[layer + 1, rows, :] + begun[layer]

    with_shifts(plan, body)


def end_kernel(plan, coeff, share, other, terms, *refs):
    *outs, one, two = refs
    place = Place(plan)
    core, s, y = place.core, place.s, place.y
    clear(plan, one, two)
    chunk = pl.ds(pl.multiple_of(place.inner(0) + TILE, TILE), plan.chunk)
    rows = pl.ds(pl.multiple_of(place.inner(TILE) + TILE, TILE), plan.width_of(TILE))
    for layer in range(plan.layers):
        one[layer + 1, rows, :] = share[layer] + other[layer]

    def write(block, field):
        @pl.when(core == block % 2)
        def _():
            for out, (dy, ds) in zip(outs, [(0, 0), *plan.others]):

                @pl.when(lax.rem(y + dy, plan.pairs) == block // 2)
                def _(out=out, ds=ds):
                    slab = lax.rem(s + ds, plan.n_s)
                    for layer in range(plan.depth):
                        value = field[1 + slab * plan.depth + layer, chunk, :]
                        out[layer] = value + terms[block // 2, slab * plan.depth + layer] if block else value

    def body(sums):
        step = stepper(plan, place, coeff, sums)
        now, spare = one, two
        write(0, now)
        for block in range(1, GROUP):
            step(now, spare, GROUP - 1 - block, RATIO)
            now, spare = spare, now
            write(block, now)

    with_shifts(plan, body)


def place_kernel(plan, *refs):
    place = Place(plan)
    out, sem, pieces = refs[-2], refs[-1], refs[:-2]
    copies = []
    for (dy, ds), piece in zip([(0, 0), *plan.others], pieces):
        y, s = place.behind(dy, ds)
        rows = pl.ds(pl.multiple_of((y * plan.n_s + s) * plan.chunk, TILE), plan.chunk)
        copies.append((piece, out.at[:, rows, :]))
    for copy in fetch(sem, copies):
        copy.wait()


def call(plan, kernel, micros, outs, scratch, *args, copies=0, whole=0, out_whole=False):
    spaces = [pltpu.HBM] * whole + [pltpu.VMEM] * (len(args) - whole)
    args = [pltpu.with_memory_space_constraint(arg, space) for arg, space in zip(args, spaces)]
    held = pltpu.HBM if out_whole else pltpu.VMEM
    needed = sum(4 * math.prod(shape) for shape in scratch)
    return pl.pallas_call(
        functools.partial(kernel, plan),
        out_shape=[held(shape, jnp.float32) for shape in outs],
        in_specs=[HBM] * whole + [VMEM] * (len(args) - whole),
        out_specs=[HBM if out_whole else VMEM] * len(outs),
        scratch_shapes=[pltpu.VMEM(shape, jnp.float32) for shape in scratch]
        + ([pltpu.SemaphoreType.DMA((copies,))] if copies else []),
        compiler_params=pltpu.CompilerParams(vmem_limit_bytes=needed + SPARE_BYTES),
        cost_estimate=pl.CostEstimate(flops=0, transcendentals=0, bytes_accessed=int(micros * 3.6e6)),
        name=kernel.__name__,
    )(*args)


def by_regions(initial, guess, diffusivity, velocity):
    plan = Plan(diffusivity.shape, lax.axis_size("tm"), lax.axis_size("space"))
    depth, lanes, width = plan.depth, plan.lanes, plan.width
    box, sides = plan.box(), plan.n_s - 1
    band, far = plan.width_of(TILE), plan.width_of(plan.far)
    window, piece = (depth, plan.wide, lanes), (depth, width, lanes)

    cuts = call(
        plan,
        first_cut_kernel,
        2,
        [piece] * sides + [window] * sides + [(depth, plan.span, lanes)] * (plan.pairs - 1),
        [],
        guess,
        initial,
        diffusivity,
        velocity,
        copies=2 * sides + plan.pairs - 1,
        whole=4,
    )
    got = [plan.send(part, ds=ds) for ds, part in enumerate(cuts[:sides], 1)]
    got += [plan.send(part, ds=ds, first=True) for ds, part in enumerate(cuts[sides : 2 * sides], 1)]
    got += [plan.send(part, dy=dy) for dy, part in enumerate(cuts[2 * sides :], 1)]
    own_sent = call(plan, second_cut_kernel, 1, [piece] * sides, [], guess, copies=sides, whole=1)
    guess_own, initial_own, coeff_own = call(
        plan, own_cut_kernel, 60, [piece, window, (4, *piece)], [], guess, initial, diffusivity, velocity, copies=4, whole=4
    )
    coeffs, inits, beside = got[:sides], got[sides : 2 * sides], got[2 * sides :]
    got = lax.optimization_barrier((*coeffs, *own_sent, *beside))
    coeffs, own_sent, beside = got[:sides], got[sides : 2 * sides], got[2 * sides :]
    mixed = call(plan, mix_kernel, 0.3, [(plan.pairs, *piece)] * sides, [], *own_sent, *beside)
    distant = [plan.send(part, ds=ds) for ds, part in enumerate(mixed, 1)]
    swapped = []
    for part in coeffs:
        flipped, part = plan.send(part, flip=True), plan.send(part, swap=True)
        swapped += [part, flipped, plan.send(part, flip=True)]
    near = []
    for index, (part, init) in enumerate(zip(coeffs, inits)):
        near += [part, *swapped[3 * index : 3 * index + 3], init]

    coeff, seed, ahead = call(
        plan,
        weight_kernel,
        3,
        [(8, plan.layers, width, lanes), box, box],
        [(sides, 4, *piece), box],
        coeff_own,
        initial_own,
        *near,
    )
    coeff, *distant = lax.optimization_barrier((coeff, *distant))
    fields, given = call(
        plan,
        field_kernel,
        0.5,
        [(plan.pairs, *box), (plan.pairs, plan.layers, plan.width_of(plan.mid), lanes)],
        [],
        guess_own,
        *beside,
        *distant,
    )
    keep, give = call(
        plan, total_kernel, 15, [(plan.side, far, lanes), (plan.side, far, lanes)], [box] * 3, coeff, ahead, fields
    )
    parts = call(
        plan,
        part_kernel,
        0.3,
        [(plan.side, plan.reach_rows(distance), lanes) for distance in range(1, plan.groups)],
        [],
        keep,
        plan.send(give, flip=True),
    )
    mine = [plan.send(parts[distance - 1], dz=distance) for distance in range(len(parts), 0, -1)]
    terms, begun = call(
        plan,
        term_kernel,
        15,
        [(plan.pairs, plan.layers, plan.chunk, lanes), (plan.layers, band, lanes)],
        [box] * 3,
        coeff,
        fields,
        plan.send(given, flip=True),
        seed,
    )
    (share,) = call(plan, start_kernel, 6, [(plan.layers, band, lanes)], [box] * 2, coeff, begun, *mine)
    results = call(
        plan,
        end_kernel,
        3,
        [(depth, plan.chunk, lanes)] * (1 + len(plan.others)),
        [box] * 2,
        coeff,
        share,
        plan.send(share, flip=True),
        terms,
    )
    back = [results[0]]
    for (dy, ds), part in zip(plan.others, results[1:]):
        back.append(plan.send(part, dy, ds))
    (out,) = call(
        plan, place_kernel, 1, [(depth, plan.rows, lanes)], [], *back, copies=len(back), out_whole=True
    )
    return out[None]


def padded_2(cells, sides, width):
    for axis, dim in sides:
        count = lax.axis_size(axis)
        ends = count - 1
        head = lax.slice_in_dim(cells, 0, width, axis=dim)
        tail = lax.slice_in_dim(cells, cells.shape[dim] - width, cells.shape[dim], axis=dim)
        cells = jnp.concatenate(
            [
                lax.ppermute(tail, axis, [(i, (i + 1) % count) for i in range(ends)]),
                cells,
                lax.ppermute(head, axis, [((i + 1) % count, i) for i in range(ends)]),
            ],
            axis=dim,
        )
    return cells


def from_behind(value, axis, steps):
    count = lax.axis_size(axis)
    first, last = (max(0, -steps), min(count, count - steps))
    return lax.ppermute(value, axis, [(source, source + steps) for source in range(first, last)])


def stencil(extended, diffus, pos_vel, neg_vel, diff_rate, adv_rate):
    center = extended[..., 1:-1, :, :]
    z_low = extended[..., :-2, :, :]
    z_high = extended[..., 2:, :, :]
    widths = [(0, 0)] * (center.ndim - 2) + [(1, 1), (1, 1)]
    padded = jnp.pad(center, widths)
    x_low = padded[..., :-2, 1:-1]
    x_high = padded[..., 2:, 1:-1]
    y_low = padded[..., 1:-1, :-2]
    y_high = padded[..., 1:-1, 2:]
    laplace = z_low + z_high + (x_low + x_high) + (y_low + y_high) - 6.0 * center
    advect = pos_vel[0] * (center - z_low) + neg_vel[0] * (z_high - center)
    advect = advect + pos_vel[1] * (center - x_low) + neg_vel[1] * (x_high - center)
    advect = advect + pos_vel[2] * (center - y_low) + neg_vel[2] * (y_high - center)
    return center + diff_rate * diffus * laplace - adv_rate * advect


def by_slabs(initial, guess, diffusivity, velocity):
    pos_vel = jnp.maximum(velocity, 0.0)
    neg_vel = jnp.minimum(velocity, 0.0)
    depth = diffusivity.shape[0]
    total_depth = depth * lax.axis_size("space")
    first_row = lax.axis_index("space") * depth
    block_index = lax.axis_index("tm")
    block_count = lax.axis_size("tm")
    state = guess[0]
    stacked = jnp.concatenate([diffusivity[None], velocity], axis=0)
    wide_coeff = padded_2(stacked, (("space", 1),), STEPS)
    wide_diff = wide_coeff[0]
    wide_pos = jnp.maximum(wide_coeff[1:], 0.0)
    wide_neg = jnp.minimum(wide_coeff[1:], 0.0)
    previous_end = from_behind(state, "tm", 1)
    starts = jnp.where(block_index == 0, initial, previous_end)
    current = padded_2(starts, (("space", 0),), STEPS)
    for step_index in range(STEPS):
        margin = STEPS - step_index - 1
        rows = depth + 2 * margin
        lower = step_index + 1
        fresh = stencil(
            current,
            wide_diff[lower : lower + rows],
            wide_pos[:, lower : lower + rows],
            wide_neg[:, lower : lower + rows],
            FINE_DIFF,
            FINE_ADV,
        )
        global_rows = first_row - margin + lax.iota(jnp.int32, rows)
        inside = (global_rows >= 0) & (global_rows < total_depth)
        current = jnp.where(inside[:, None, None], fresh, 0.0)
    residue = current - state

    def sweep_turn(index, carry):
        previous = from_behind(carry, "tm", 1)
        beside_all = padded_2(previous, (("space", 0),), 1)
        return stencil(beside_all, diffusivity, pos_vel, neg_vel, RATIO * FINE_DIFF, RATIO * FINE_ADV) + residue

    correction = lax.fori_loop(0, block_count, sweep_turn, jnp.zeros_like(state))
    state = state + correction
    return state[None]


def fits(plan):
    if plan.n_t % (2 * GROUP) or plan.layers % 2 or plan.rows % (plan.pairs * plan.n_s * TILE) or plan.lanes != LANES:
        return False
    return plan.n_s > 1 and 4 * 24 * plan.layers * plan.width * plan.lanes <= VMEM_BYTES


def per_device(initial, guess, diffusivity, velocity):
    shape, n_t, n_s = diffusivity.shape, lax.axis_size("tm"), lax.axis_size("space")
    way = by_regions if n_t > GROUP and fits(Plan(shape, n_t, n_s)) else by_slabs
    return way(initial, guess, diffusivity, velocity)


def solution(mesh):
    in_specs = (
        P("space", None, None),
        P("tm", "space", None, None),
        P("space", None, None),
        P(None, "space", None, None),
    )
    out_specs = P("tm", "space", None, None)
    return jax.shard_map(per_device, mesh=mesh, in_specs=in_specs, out_specs=out_specs, check_vma=False)
```
